32 devices in a mesh: group: 2 (over x), tok: 16 (over z, y, core).
Axes of the slice: x: 2, y: 2, z: 4, core: 2. Of those that a mesh axis runs over, the one named last changes fastest.
Arguments:
- initial_guess: float32 [512, 16, 128], P(('group', 'tok')), parts along dimension 0, may hold values from -6 to 6
- noise_draws: float32 [512, 16, 128], P(('group', 'tok')), parts along dimension 0, may hold values from -6 to 6
- drift_state: float32 [16], replicated, may hold values from 0 to 0.15
- drift_denoise: float32 [16], replicated, may hold values from -0.4 to -0.15
- noise_scale: float32 [16], replicated, may hold values from 0.05 to 0.3
- modulation: float32 [16, 8, 1152], replicated, may hold values from -3 to 3
- embed_weight: bfloat16 [16, 1152], replicated, may hold values from -1.5 to 1.5
- space_input: bfloat16 [1152, 1728], replicated, may hold values from -0.1875 to 0.1875
- space_output: bfloat16 [576, 1152], replicated, may hold values from -0.25 to 0.25
- time_input: bfloat16 [1152, 1728], replicated, may hold values from -0.1875 to 0.1875
- time_output: bfloat16 [576, 1152], replicated, may hold values from -0.25 to 0.25
- final_weight: bfloat16 [1152, 16], replicated, may hold values from -0.1875 to 0.1875
Outputs:
- next_states: float32 [512, 16, 128], P(('group', 'tok')), parts along dimension 0
The draws below stay inside these ranges and needn't reach their ends.
There are 2 independent parts, one for each index of `group`. The reference program is written for one: setup_inputs(seed, part) draws one part's arguments, and reference() takes and returns one part's arrays. A program takes and returns all parts, laid end to end along the dimension named above; an argument that names none is the same for every part. Nothing has to cross between parts.
All inputs are finite; a program needn't handle non-finite values.
Results may differ from the reference program's by a relative error of at most 0.006.
Values may be sent and summed in bfloat16 or wider, within the bound.
No kernel may reach another device: no remote copies, remote signals or barrier semaphores. Data moves between devices by JAX's collectives and lax.ppermute only.
A program may use at most 128 MiB of HBM per device.

```python
import jax
import jax.numpy as jnp
from jax import lax

D = 1152
HEADS = 8
HD = 72
LCH = 16
F = 16
P_SIZE = 16
ITERS = 2
HW = 128
INNER = 576
ROWS = 256


def steps_of(stream_key, shape, cuts, least, largest):
    gain, own = 1.0, jax.random.fold_in(stream_key, 6)
    for position, shards_of in cuts:
        steps = jnp.exp(jax.random.uniform(jax.random.fold_in(own, position), (shards_of,), jnp.float32, least / len(cuts), largest / len(cuts)))
        gain = gain * jnp.repeat(steps, shape[position] // shards_of).reshape([-1 if axis == position else 1 for axis in range(len(shape))])
    return gain


def centred(key, shape, spread, bound, shards=(), kind=jnp.bfloat16):
    values = spread * jax.random.normal(key, shape, jnp.float32)
    if shards:
        values = values * steps_of(key, shape, shards, -0.22, 0.18)
    return jnp.clip(values, -bound, bound).astype(kind)


def setup_inputs(seed: int = 0, part: int = 0) -> dict:
    arg_keys = jax.random.split(jax.random.key(seed), 13)
    part_splits = jax.random.split(jax.random.fold_in(arg_keys[12], part), 13)
    return {
        "initial_guess": centred(part_splits[0], (ROWS, LCH, HW), 1.0, 6.0, ((0, 16),), jnp.float32),
        "noise_draws": centred(part_splits[1], (ROWS, LCH, HW), 1.0, 6.0, ((0, 16),), jnp.float32),
        "drift_state": jnp.clip(jax.random.uniform(arg_keys[2], (P_SIZE,), jnp.float32, 0.0, 0.15), 0.0, 0.15),
        "drift_denoise": jnp.clip(jax.random.uniform(arg_keys[3], (P_SIZE,), jnp.float32, -0.4, -0.15), -0.4, -0.15),
        "noise_scale": jnp.clip(jax.random.uniform(arg_keys[4], (P_SIZE,), jnp.float32, 0.05, 0.3), 0.05, 0.3),
        "modulation": centred(arg_keys[5], (P_SIZE, 8, D), 0.4, 3.0, (), jnp.float32),
        "embed_weight": centred(arg_keys[6], (LCH, D), LCH ** -0.5, 1.5),
        "space_input": centred(arg_keys[7], (D, 3 * INNER), D ** -0.5, 0.1875),
        "space_output": centred(arg_keys[8], (INNER, D), INNER ** -0.5, 0.25),
        "time_input": centred(arg_keys[9], (D, 3 * INNER), D ** -0.5, 0.1875),
        "time_output": centred(arg_keys[10], (INNER, D), INNER ** -0.5, 0.25),
        "final_weight": centred(arg_keys[11], (D, LCH), D ** -0.5, 0.1875),
    }


def layer_norm(values):
    center = values - lax.optimization_barrier(jnp.mean(values, -1, keepdims=True))
    return center * lax.rsqrt(lax.optimization_barrier(jnp.mean(center * center, -1, keepdims=True)) + 1e-06)

def head_norm(values):
    return values * lax.rsqrt(lax.optimization_barrier(jnp.mean(values * values, -1, keepdims=True)) + 1e-06)

def attention_mix(normed, input_weight, output_weight):
    batches, length, feature_width = normed.shape
    packed = jnp.dot(normed.reshape(-1, feature_width), input_weight, preferred_element_type=jnp.float32)
    packed = packed.reshape(batches, length, 3, HEADS, HD)
    queries = head_norm(packed[:, :, 0]).astype(jnp.bfloat16)
    key_rows = head_norm(packed[:, :, 1]).astype(jnp.bfloat16)
    value_rows = packed[:, :, 2].astype(jnp.bfloat16)
    scores = jnp.einsum('blhe,bmhe->bhlm', queries.astype(jnp.float32), key_rows.astype(jnp.float32)) * HD ** (-0.5)
    weights = jnp.exp(scores)
    weights = (weights / lax.optimization_barrier(jnp.sum(weights, -1, keepdims=True))).astype(jnp.bfloat16)
    attended = jnp.einsum('bhlm,bmhe->blhe', weights.astype(jnp.float32), value_rows.astype(jnp.float32)).astype(jnp.bfloat16)
    result = jnp.dot(attended.reshape(-1, HEADS * HD), output_weight, preferred_element_type=jnp.float32)
    return result.reshape(batches, length, feature_width)

def denoiser(latent, modulation_row, embed_weight, space_input, space_output, time_input, time_output, final_weight):
    embedded = jnp.einsum('fch,cd->fhd', latent.astype(jnp.bfloat16).astype(jnp.float32), embed_weight.astype(jnp.float32))
    normed = (layer_norm(embedded) * (1.0 + modulation_row[1]) + modulation_row[0]).astype(jnp.bfloat16)
    after_space = (embedded + modulation_row[2] * attention_mix(normed, space_input, space_output)).astype(jnp.bfloat16)
    after_space = lax.optimization_barrier(after_space)
    hidden = jnp.swapaxes(after_space, 0, 1).astype(jnp.float32)
    normed = (layer_norm(hidden) * (1.0 + modulation_row[4]) + modulation_row[3]).astype(jnp.bfloat16)
    after_time = (hidden + modulation_row[5] * attention_mix(normed, time_input, time_output)).astype(jnp.bfloat16)
    after_time = lax.optimization_barrier(after_time).astype(jnp.float32)
    normed = (layer_norm(after_time) * (1.0 + modulation_row[7]) + modulation_row[6]).astype(jnp.bfloat16)
    return jnp.einsum('hfd,dc->fch', normed.astype(jnp.float32), final_weight.astype(jnp.float32))

def reference(initial_guess, noise_draws, drift_state, drift_denoise, noise_scale, modulation, embed_weight, space_input, space_output, time_input, time_output, final_weight):
    latent = initial_guess.reshape(P_SIZE, F, LCH, HW)
    fresh_noise = noise_draws.reshape(P_SIZE, F, LCH, HW)
    leading = (jnp.arange(P_SIZE) == 0)[:, None, None, None]
    rate_state = drift_state[:, None, None, None]
    rate_denoise = drift_denoise[:, None, None, None]
    rate_noise = noise_scale[:, None, None, None]
    running = latent
    for iteration in range(ITERS):
        predicted = lax.map(lambda paired: denoiser(paired[0], paired[1], embed_weight, space_input, space_output, time_input, time_output, final_weight), (latent, modulation))
        increment = rate_state * latent + rate_denoise * predicted + rate_noise * fresh_noise
        increment = jnp.where(leading, increment + latent, increment)
        running = jnp.cumsum(increment, axis=0)
        latent = jnp.concatenate([latent[:1], running[:-1]], axis=0)
    return running.reshape(ROWS, LCH, HW)
```

```python
import functools
import math

import jax
import jax.numpy as jnp
from jax import lax
from jax.experimental import pallas as pl
from jax.experimental.pallas import tpu as pltpu
from jax.sharding import PartitionSpec as P

HEADS = 8
ITERS = 2
LANES = 128
ROWS8 = 8
F32 = jnp.float32
BF16 = jnp.bfloat16


def layer_norm(values):
    center = values - jnp.mean(values, -1, keepdims=True)
    return center * lax.rsqrt(jnp.mean(center * center, -1, keepdims=True) + 1e-06)


def head_spans(lane_start, lanes, head_size):
    spans = []
    for head in range(HEADS):
        first = max(head * head_size, lane_start) - lane_start
        last = min((head + 1) * head_size, lane_start + lanes) - lane_start
        if first < last:
            spans.append((head, first, last))
    return spans


def lane_mask(shape, first, last):
    lanes = lax.broadcasted_iota(jnp.int32, shape, len(shape) - 1)
    return (lanes >= first) & (lanes < last)


def normed_heads(values, head_size, scale):
    rows, width = values.shape
    tiles = [values[:, at : at + LANES] for at in range(0, width, LANES)]
    totals = [None] * HEADS
    for index, tile in enumerate(tiles):
        square = tile * tile
        for head, first, last in head_spans(index * LANES, LANES, head_size):
            part = jnp.where(lane_mask((1, LANES), first, last), square, 0.0)
            totals[head] = part if totals[head] is None else totals[head] + part
    rates = [
        lax.rsqrt(jnp.sum(total, -1, keepdims=True) * (1.0 / head_size) + 1e-06) * scale
        for total in totals
    ]
    normed = []
    for index, tile in enumerate(tiles):
        spans = head_spans(index * LANES, LANES, head_size)
        rate = rates[spans[-1][0]]
        for head, first, last in reversed(spans[:-1]):
            rate = jnp.where(lane_mask((1, LANES), 0, last), rates[head], rate)
        normed.append((tile * rate).astype(BF16))
    return normed


def attention(normed, input_weight, output_weight, group_rows, same_position):
    rows = normed.shape[0]
    inner = output_weight.shape[0]
    head_size = inner // HEADS
    wide = -(-inner // LANES) * LANES
    packed = jnp.dot(normed, input_weight, preferred_element_type=F32)
    queries = normed_heads(
        packed[:, :wide], head_size, head_size ** (-0.5) * math.log2(math.e)
    )
    key_rows = normed_heads(packed[:, inner : inner + wide], head_size, 1.0)
    value_rows = packed[:, 2 * inner :].astype(BF16)
    attended_groups = []
    for start in range(0, rows, group_rows):
        stop = start + group_rows
        attended = [None] * (wide // LANES)
        for pair in range(HEADS // 2):
            base = 2 * pair * head_size // LANES
            tiles = [base, base + 1]
            keys = jnp.concatenate([key_rows[t][start:stop] for t in tiles], 1)
            window = jnp.concatenate([queries[t][start:stop] for t in tiles], 1)
            low = base * LANES
            high = min(low + 2 * LANES, inner)
            values = value_rows[start:stop, low:high]
            weights, stacked, rates = [], [], []
            for head in (2 * pair, 2 * pair + 1):
                first, last = head * head_size - low, (head + 1) * head_size - low
                query = jnp.where(
                    lane_mask((1, 2 * LANES), first, last), window, jnp.zeros_like(window)
                )
                scores = lax.dot_general(
                    query, keys, (((1,), (1,)), ((), ())), preferred_element_type=F32
                )
                weight = jnp.exp2(scores)
                if same_position is not None:
                    weight = weight * same_position
                rates.append(1.0 / jnp.sum(weight, -1, keepdims=True))
                weights.append(weight.astype(BF16))
                stacked.append(
                    jnp.where(
                        lane_mask((1, high - low), first, last), values, jnp.zeros_like(values)
                    )
                )
            mixed = jnp.dot(
                jnp.concatenate(weights, 1),
                jnp.concatenate(stacked, 0),
                preferred_element_type=F32,
            )
            border = (2 * pair + 1) * head_size - low
            mixed = mixed * jnp.where(
                lane_mask((1, high - low), 0, border), rates[0], rates[1]
            )
            for t in tiles:
                at = t * LANES - low
                part = mixed[:, at : min(at + LANES, high - low)]
                attended[t] = part if attended[t] is None else attended[t] + part
        attended_groups.append(
            jnp.concatenate([part.astype(BF16) for part in attended], 1)
        )
    attended = (
        jnp.concatenate(attended_groups, 0) if len(attended_groups) > 1 else attended_groups[0]
    )
    return jnp.dot(attended, output_weight, preferred_element_type=F32)


def space_step(at, frames, latent, embed, rows_of, input_weight, output_weight, out):
    spatial = latent.shape[2]
    embedded = jnp.concatenate(
        [
            lax.dot_general(
                latent[at + index].astype(BF16),
                embed[...],
                (((0,), (0,)), ((), ())),
                preferred_element_type=F32,
            )
            for index in range(frames)
        ],
        0,
    )
    normed = (layer_norm(embedded) * (1.0 + rows_of[1:2]) + rows_of[0:1]).astype(BF16)
    mixed = attention(normed, input_weight[...], output_weight[...], spatial, None)
    after = embedded + rows_of[2:3] * mixed
    for index in range(frames):
        out[at + index] = after[index * spatial : (index + 1) * spatial].astype(out.dtype)


def time_step(at, count, after, rows_of, input_weight, output_weight, final, out, same_position):
    frames, width = after.shape[0], after.shape[2]
    hidden = jnp.concatenate(
        [
            after[:, pl.ds(pl.multiple_of(at + index * ROWS8, ROWS8), ROWS8), :].reshape(
                frames * ROWS8, width
            )
            for index in range(count)
        ],
        0,
    ).astype(F32)
    normed = (layer_norm(hidden) * (1.0 + rows_of[4:5]) + rows_of[3:4]).astype(BF16)
    mixed = attention(
        normed, input_weight[...], output_weight[...], frames * ROWS8, same_position
    )
    settled = hidden + rows_of[5:6] * mixed
    normed = (layer_norm(settled) * (1.0 + rows_of[7:8]) + rows_of[6:7]).astype(BF16)
    predicted = jnp.dot(normed, final[...], preferred_element_type=F32)
    for index in range(count):
        part = predicted[index * frames * ROWS8 : (index + 1) * frames * ROWS8]
        out[:, pl.ds(pl.multiple_of(at + index * ROWS8, ROWS8), ROWS8), :] = part.reshape(
            frames, ROWS8, part.shape[1]
        )


def same_position_mask(frames):
    rows = frames * ROWS8
    row = lax.broadcasted_iota(jnp.int32, (rows, rows), 0) % ROWS8
    column = lax.broadcasted_iota(jnp.int32, (rows, rows), 1) % ROWS8
    return jnp.where(row == column, 1.0, 0.0).astype(F32)


def both(blocks):
    return 2 if blocks % 2 == 0 else 1


def run_space(latent, embed, rows_of, input_weight, output_weight, out):
    frames = latent.shape[0]
    step = both(frames)

    @pl.loop(0, frames // step)
    def _(index):
        space_step(index * step, step, latent, embed, rows_of, input_weight, output_weight, out)


def run_time(after, rows_of, input_weight, output_weight, final, out):
    frames, positions = after.shape[0], after.shape[1]
    step = both(positions // ROWS8)
    same_position = same_position_mask(frames)

    @pl.loop(0, positions // (step * ROWS8))
    def _(index):
        time_step(
            index * step * ROWS8, step, after, rows_of, input_weight, output_weight, final, out,
            same_position,
        )


def fused_kernel(
    latent, rows_of, embed, space_in_hbm, space_out_hbm, time_in_hbm, time_out_hbm, final,
    predicted, space_in, space_out, time_in, time_out, after, staged, sems,
):
    copies = [
        pltpu.make_async_copy(source, target, sems.at[index])
        for index, (source, target) in enumerate(
            (
                (space_in_hbm, space_in),
                (space_out_hbm, space_out),
                (time_in_hbm, time_in),
                (time_out_hbm, time_out),
            )
        )
    ]
    for copy in copies:
        copy.start()
    copies[0].wait()
    copies[1].wait()
    run_space(latent, embed, rows_of, space_in, space_out, after)
    copies[2].wait()
    copies[3].wait()
    run_time(after, rows_of, time_in, time_out, final, staged)
    for frame in range(latent.shape[0]):
        predicted[frame] = staged[frame].T


def space_kernel(latent, rows_of, embed, space_in, space_out, after):
    run_space(latent, embed, rows_of, space_in, space_out, after)


def time_kernel(after, rows_of, time_in, time_out, final, predicted):
    run_time(after, rows_of, time_in, time_out, final, predicted)


def vmem(count):
    return [pl.BlockSpec(memory_space=pltpu.VMEM)] * count


PARAMS = dict(compiler_params=pltpu.CompilerParams(vmem_limit_bytes=56 * 2**20))


def denoise_fused(latent, rows_of, embed, space_in, space_out, time_in, time_out, final):
    frames, channels, spatial = latent.shape
    width = embed.shape[1]
    return pl.pallas_call(
        fused_kernel,
        out_shape=jax.ShapeDtypeStruct(latent.shape, F32),
        in_specs=vmem(3) + [pl.BlockSpec(memory_space=pl.ANY)] * 4 + vmem(1),
        out_specs=vmem(1)[0],
        scratch_shapes=[
            pltpu.VMEM(space_in.shape, BF16),
            pltpu.VMEM(space_out.shape, BF16),
            pltpu.VMEM(time_in.shape, BF16),
            pltpu.VMEM(time_out.shape, BF16),
            pltpu.VMEM((frames, spatial, width), F32),
            pltpu.VMEM((frames, spatial, channels), F32),
            pltpu.SemaphoreType.DMA((4,)),
        ],
        name="denoise",
        **PARAMS,
    )(latent, rows_of, embed, space_in, space_out, time_in, time_out, final)


def denoise_split(latent, rows_of, embed, space_in, space_out, time_in, time_out, final, peers):
    frames, channels, spatial = latent.shape
    width = embed.shape[1]
    after = pl.pallas_call(
        space_kernel,
        out_shape=jax.ShapeDtypeStruct((frames, spatial, width), BF16),
        in_specs=vmem(5),
        out_specs=vmem(1)[0],
        name="space",
        **PARAMS,
    )(latent, rows_of, embed, space_in, space_out)
    after = lax.all_to_all(
        after, "tok", split_axis=1, concat_axis=0, tiled=True, axis_index_groups=peers
    )
    predicted = pl.pallas_call(
        time_kernel,
        out_shape=jax.ShapeDtypeStruct(after.shape[:2] + (channels,), F32),
        in_specs=vmem(5),
        out_specs=vmem(1)[0],
        name="time",
        **PARAMS,
    )(after.astype(F32), rows_of, time_in, time_out, final)
    predicted = lax.all_to_all(
        predicted, "tok", split_axis=0, concat_axis=1, tiled=True, axis_index_groups=peers
    )
    return jnp.swapaxes(predicted, 1, 2)


def sum_before(values, timesteps, groups):
    before = jnp.zeros_like(values)
    reach = 1
    while reach < timesteps:
        moves = [
            (step * groups + block, (step + reach) * groups + block)
            for step in range(timesteps - reach)
            for block in range(groups)
        ]
        held = (values + before).astype(BF16)
        before = before + lax.ppermute(held, "tok", moves).astype(F32)
        reach *= 2
    return before


def body(
    initial_guess,
    noise_draws,
    drift_state,
    drift_denoise,
    noise_scale,
    modulation,
    embed_weight,
    space_input,
    space_output,
    time_input,
    time_output,
    final_weight,
):
    timesteps = modulation.shape[0]
    devices = lax.axis_size("tok")
    groups = devices // timesteps
    timestep = lax.axis_index("tok") // groups
    leading = timestep == 0
    rows_of = lax.dynamic_index_in_dim(modulation, timestep, 0, keepdims=False)
    rate_state = lax.dynamic_index_in_dim(drift_state, timestep, 0, keepdims=False)
    rate_denoise = lax.dynamic_index_in_dim(drift_denoise, timestep, 0, keepdims=False)
    rate_noise = lax.dynamic_index_in_dim(noise_scale, timestep, 0, keepdims=False)
    if groups == 1:
        denoise = denoise_fused
    else:
        peers = [[step * groups + block for block in range(groups)] for step in range(timesteps)]
        denoise = functools.partial(denoise_split, peers=peers)
    weights = (embed_weight, space_input, space_output, time_input, time_output, final_weight)
    latent = initial_guess
    result = initial_guess
    for _ in range(ITERS):
        predicted = denoise(latent, rows_of, *weights)
        increment = rate_state * latent + rate_denoise * predicted + rate_noise * noise_draws
        increment = jnp.where(leading, increment + latent, increment)
        before = sum_before(increment, timesteps, groups)
        result = before + increment
        latent = jnp.where(leading, latent, before)
    return result


def solution(mesh):
    rows = P(("group", "tok"), None, None)
    placed = (rows, rows) + (P(),) * 10
    return jax.shard_map(
        body, mesh=mesh, in_specs=placed, out_specs=rows, check_vma=False
    )
```

```python
import functools
import math

import jax
import jax.numpy as jnp
from jax import lax
from jax.experimental import pallas as pl
from jax.experimental.pallas import tpu as pltpu
from jax.sharding import PartitionSpec as P

HEADS = 8
ITERS = 2
ROWS8 = 8
ROWS16 = 16
F32 = jnp.float32
BF16 = jnp.bfloat16


def layer_norm(values):
    center = values - jnp.mean(values, -1, keepdims=True)
    return center * lax.rsqrt(jnp.mean(center * center, -1, keepdims=True) + 1e-06)


def normed_head(values, head_size, scale):
    total = jnp.sum(values * values, 0, keepdims=True)
    return values * (lax.rsqrt(total * (1.0 / head_size) + 1e-06) * scale)


def padded(values, fill):
    rows, columns = values.shape
    extra = ROWS16 - rows % ROWS16
    return jnp.concatenate([values, jnp.full((extra, columns), fill, F32)], 0).astype(BF16)


def attention(normed, input_turned, output_weight, group_rows, same_position):
    tokens = normed.shape[0]
    inner = output_weight.shape[0]
    head_size = inner // HEADS
    packed = lax.dot_general(
        input_turned, normed, (((1,), (1,)), ((), ())), preferred_element_type=F32
    )
    starts = range(0, tokens, group_rows)
    attended = [[] for _ in starts]
    for head in range(HEADS):
        at = head * head_size
        query = packed[at : at + head_size]
        key = packed[inner + at : inner + at + head_size]
        value = packed[2 * inner + at : 2 * inner + at + head_size]
        query = padded(
            normed_head(query, head_size, head_size ** (-0.5) * math.log2(math.e)), 0.0
        )
        key = padded(normed_head(key, head_size, 1.0), 0.0)
        value = padded(value, 1.0)
        for group, start in enumerate(starts):
            columns = slice(start, start + group_rows)
            scores = lax.dot_general(
                key[:, columns],
                query[:, columns],
                (((0,), (0,)), ((), ())),
                preferred_element_type=F32,
            )
            weights = jnp.exp2(scores).astype(BF16)
            if same_position is not None:
                weights = weights * same_position
            mixed = jnp.dot(value[:, columns], weights, preferred_element_type=F32)
            rate = 1.0 / mixed[head_size : head_size + ROWS8]
            parts = mixed[:head_size].reshape(head_size // ROWS8, ROWS8, group_rows) * rate[None]
            attended[group].append(parts.reshape(head_size, group_rows))
    attended = jnp.concatenate([jnp.concatenate(part, 0) for part in attended], 1).astype(BF16)
    return lax.dot_general(
        attended, output_weight, (((0,), (0,)), ((), ())), preferred_element_type=F32
    )


def space_step(at, frames, latent, embed, rows_of, input_weight, output_weight, out):
    spatial = latent.shape[2]
    embedded = jnp.concatenate(
        [
            lax.dot_general(
                latent[at + index].astype(BF16),
                embed[...],
                (((0,), (0,)), ((), ())),
                preferred_element_type=F32,
            )
            for index in range(frames)
        ],
        0,
    )
    normed = (layer_norm(embedded) * (1.0 + rows_of[1:2]) + rows_of[0:1]).astype(BF16)
    mixed = attention(normed, input_weight[...], output_weight[...], spatial, None)
    after = embedded + rows_of[2:3] * mixed
    for index in range(frames):
        out[at + index] = after[index * spatial : (index + 1) * spatial].astype(out.dtype)


def time_step(at, count, after, rows_of, input_weight, output_weight, final, out, same_position):
    frames, width = after.shape[0], after.shape[2]
    hidden = jnp.concatenate(
        [
            after[:, pl.ds(pl.multiple_of(at + index * ROWS8, ROWS8), ROWS8), :].reshape(
                frames * ROWS8, width
            )
            for index in range(count)
        ],
        0,
    ).astype(F32)
    normed = (layer_norm(hidden) * (1.0 + rows_of[4:5]) + rows_of[3:4]).astype(BF16)
    mixed = attention(
        normed, input_weight[...], output_weight[...], frames * ROWS8, same_position
    )
    settled = hidden + rows_of[5:6] * mixed
    normed = (layer_norm(settled) * (1.0 + rows_of[7:8]) + rows_of[6:7]).astype(BF16)
    predicted = lax.dot_general(
        normed, final[...], (((1,), (1,)), ((), ())), preferred_element_type=F32
    )
    for index in range(count):
        part = predicted[index * frames * ROWS8 : (index + 1) * frames * ROWS8]
        out[:, pl.ds(pl.multiple_of(at + index * ROWS8, ROWS8), ROWS8), :] = part.reshape(
            frames, ROWS8, part.shape[1]
        )


def same_position_mask(frames):
    rows = frames * ROWS8
    row = lax.broadcasted_iota(jnp.int32, (rows, rows), 0) % ROWS8
    column = lax.broadcasted_iota(jnp.int32, (rows, rows), 1) % ROWS8
    return jnp.where(row == column, 1.0, 0.0).astype(BF16)


def both(blocks):
    return 2 if blocks % 2 == 0 else 1


def run_space(latent, embed, rows_of, input_weight, output_weight, out):
    frames = latent.shape[0]
    step = both(frames)

    @pl.loop(0, frames // step)
    def _(index):
        space_step(index * step, step, latent, embed, rows_of, input_weight, output_weight, out)


def run_time(after, rows_of, input_weight, output_weight, final, out):
    frames, positions = after.shape[0], after.shape[1]
    step = both(positions // ROWS8)
    same_position = same_position_mask(frames)

    @pl.loop(0, positions // (step * ROWS8))
    def _(index):
        time_step(
            index * step * ROWS8, step, after, rows_of, input_weight, output_weight, final, out,
            same_position,
        )


def fused_kernel(
    timestep, rate_state, rate_denoise, rate_noise, latent, noise, modulation, embed,
    space_in_hbm, space_out_hbm, time_in_hbm, time_out_hbm, final, increment, rounded,
    rows_of, space_in, space_out, time_in, time_out, after, staged, sems,
):
    own = timestep[0]
    copies = [
        pltpu.make_async_copy(source, target, sems.at[index])
        for index, (source, target) in enumerate(
            (
                (modulation.at[own], rows_of),
                (space_in_hbm, space_in),
                (space_out_hbm, space_out),
                (time_in_hbm, time_in),
                (time_out_hbm, time_out),
            )
        )
    ]
    for copy in copies:
        copy.start()
    for copy in copies[:3]:
        copy.wait()
    run_space(latent, embed, rows_of, space_in, space_out, after)
    for copy in copies[3:]:
        copy.wait()
    run_time(after, rows_of, time_in, time_out, final, staged)
    keep = rate_state[own] + jnp.where(own == 0, 1.0, 0.0)
    for frame in range(latent.shape[0]):
        value = (
            keep * latent[frame]
            + rate_denoise[own] * staged[frame].T
            + rate_noise[own] * noise[frame]
        )
        increment[frame] = value
        rounded[frame] = value.astype(BF16)


def space_kernel(latent, rows_of, embed, space_in, space_out, after):
    run_space(latent, embed, rows_of, space_in, space_out, after)


def time_kernel(after, rows_of, time_in, time_out, final, predicted):
    run_time(after, rows_of, time_in, time_out, final, predicted)


def vmem(count):
    return [pl.BlockSpec(memory_space=pltpu.VMEM)] * count


PARAMS = dict(compiler_params=pltpu.CompilerParams(vmem_limit_bytes=56 * 2**20))


def scalars(count):
    return [pl.BlockSpec(memory_space=pltpu.SMEM)] * count


def step_fused(timestep, rates, latent, noise, modulation, weights):
    frames, channels, spatial = latent.shape
    embed, space_in, space_out, time_in, time_out, final = weights
    width = embed.shape[1]
    return pl.pallas_call(
        fused_kernel,
        out_shape=[
            jax.ShapeDtypeStruct(latent.shape, F32),
            jax.ShapeDtypeStruct(latent.shape, BF16),
        ],
        in_specs=scalars(4)
        + vmem(2)
        + [pl.BlockSpec(memory_space=pl.ANY)]
        + vmem(1)
        + [pl.BlockSpec(memory_space=pl.ANY)] * 4
        + vmem(1),
        out_specs=vmem(2),
        scratch_shapes=[
            pltpu.VMEM(modulation.shape[1:], F32),
            pltpu.VMEM(space_in.shape, BF16),
            pltpu.VMEM(space_out.shape, BF16),
            pltpu.VMEM(time_in.shape, BF16),
            pltpu.VMEM(time_out.shape, BF16),
            pltpu.VMEM((frames, spatial, width), F32),
            pltpu.VMEM((frames, spatial, channels), F32),
            pltpu.SemaphoreType.DMA((5,)),
        ],
        name="denoise",
        **PARAMS,
    )(
        timestep, *rates, latent, noise, modulation, embed, space_in, space_out, time_in,
        time_out, final,
    )


def step_split(timestep, rates, latent, noise, modulation, weights, peers):
    frames, channels, spatial = latent.shape
    embed, space_in, space_out, time_in, time_out, final = weights
    width = embed.shape[1]
    own = timestep[0]
    rows_of = lax.dynamic_index_in_dim(modulation, own, 0, keepdims=False)
    after = pl.pallas_call(
        space_kernel,
        out_shape=jax.ShapeDtypeStruct((frames, spatial, width), BF16),
        in_specs=vmem(5),
        out_specs=vmem(1)[0],
        name="space",
        **PARAMS,
    )(latent, rows_of, embed, space_in, space_out)
    after = lax.all_to_all(
        after, "tok", split_axis=1, concat_axis=0, tiled=True, axis_index_groups=peers
    )
    predicted = pl.pallas_call(
        time_kernel,
        out_shape=jax.ShapeDtypeStruct(after.shape[:2] + (channels,), F32),
        in_specs=vmem(5),
        out_specs=vmem(1)[0],
        name="time",
        **PARAMS,
    )(after.astype(F32), rows_of, time_in, time_out, final)
    predicted = lax.all_to_all(
        predicted, "tok", split_axis=0, concat_axis=1, tiled=True, axis_index_groups=peers
    )
    rate_state, rate_denoise, rate_noise = (rate[own] for rate in rates)
    increment = (
        (rate_state + jnp.where(own == 0, 1.0, 0.0)) * latent
        + rate_denoise * jnp.swapaxes(predicted, 1, 2)
        + rate_noise * noise
    )
    return increment, increment.astype(BF16)


RADIX = 4


def sum_before(values, held, timesteps, groups):
    before = jnp.zeros_like(values)
    reach = 1
    while reach < timesteps:
        arrived = []
        for back in range(reach, min(reach * RADIX, timesteps), reach):
            moves = [
                (step * groups + block, (step + back) * groups + block)
                for step in range(timesteps - back)
                for block in range(groups)
            ]
            arrived.append(lax.ppermute(held, "tok", moves))
        for part in arrived:
            before = before + part.astype(F32)
        held = (values + before).astype(BF16)
        reach *= RADIX
    return before


def body(
    initial_guess,
    noise_draws,
    drift_state,
    drift_denoise,
    noise_scale,
    modulation,
    embed_weight,
    space_input,
    space_output,
    time_input,
    time_output,
    final_weight,
):
    timesteps = modulation.shape[0]
    devices = lax.axis_size("tok")
    groups = devices // timesteps
    timestep = lax.axis_index("tok") // groups
    leading = timestep == 0
    own = timestep.astype(jnp.int32).reshape(1)
    if groups == 1:
        step = step_fused
    else:
        peers = [[row * groups + block for block in range(groups)] for row in range(timesteps)]
        step = functools.partial(step_split, peers=peers)
    rates = (drift_state, drift_denoise, noise_scale)
    weights = (
        embed_weight, space_input.T, space_output, time_input.T, time_output, final_weight.T
    )
    latent = initial_guess
    result = initial_guess
    for _ in range(ITERS):
        increment, rounded = step(own, rates, latent, noise_draws, modulation, weights)
        before = sum_before(increment, rounded, timesteps, groups)
        result = before + increment
        latent = jnp.where(leading, latent, before)
    return result


def solution(mesh):
    rows = P(("group", "tok"), None, None)
    placed = (rows, rows) + (P(),) * 10
    return jax.shard_map(
        body, mesh=mesh, in_specs=placed, out_specs=rows, check_vma=False
    )
```

```python
import functools
import math

import jax
import jax.numpy as jnp
from jax import lax
from jax.experimental import pallas as pl
from jax.experimental.pallas import tpu as pltpu
from jax.sharding import PartitionSpec as P

HEADS = 8
ITERS = 2
ROWS8 = 8
ROWS16 = 16
F32 = jnp.float32
BF16 = jnp.bfloat16


def layer_norm(values):
    center = values - jnp.mean(values, -1, keepdims=True)
    return center * lax.rsqrt(jnp.mean(center * center, -1, keepdims=True) + 1e-06)


def normed_head(values, head_size, scale):
    total = jnp.sum(values * values, 0, keepdims=True)
    return values * (lax.rsqrt(total * (1.0 / head_size) + 1e-06) * scale)


def padded(values, fill):
    rows, columns = values.shape
    extra = ROWS16 - rows % ROWS16
    return jnp.concatenate([values, jnp.full((extra, columns), fill, F32)], 0).astype(BF16)


def attention(normed, input_turned, output_weight, group_rows, same_position):
    tokens = normed.shape[0]
    inner = output_weight.shape[0]
    head_size = inner // HEADS
    packed = jnp.dot(input_turned, normed.T, preferred_element_type=F32)
    starts = range(0, tokens, group_rows)
    attended = [[] for _ in starts]
    for head in range(HEADS):
        at = head * head_size
        query = packed[at : at + head_size]
        key = packed[inner + at : inner + at + head_size]
        value = packed[2 * inner + at : 2 * inner + at + head_size]
        query = padded(
            normed_head(query, head_size, head_size ** (-0.5) * math.log2(math.e)), 0.0
        )
        key = padded(normed_head(key, head_size, 1.0), 0.0)
        value = padded(value, 1.0)
        for group, start in enumerate(starts):
            columns = slice(start, start + group_rows)
            scores = jnp.dot(key[:, columns].T, query[:, columns], preferred_element_type=F32)
            weights = jnp.exp2(scores).astype(BF16)
            if same_position is not None:
                weights = weights * same_position
            mixed = jnp.dot(value[:, columns], weights, preferred_element_type=F32)
            rate = 1.0 / mixed[head_size : head_size + ROWS8]
            parts = mixed[:head_size].reshape(head_size // ROWS8, ROWS8, group_rows) * rate[None]
            attended[group].append(parts.reshape(head_size, group_rows))
    attended = jnp.concatenate([jnp.concatenate(part, 0) for part in attended], 1).astype(BF16)
    return jnp.dot(attended.T, output_weight, preferred_element_type=F32)


def space_step(at, frames, latent, embed, rows_of, input_weight, output_weight, out):
    spatial = latent.shape[2]
    embedded = jnp.concatenate(
        [
            lax.dot_general(
                latent[at + index].astype(BF16),
                embed[...],
                (((0,), (0,)), ((), ())),
                preferred_element_type=F32,
            )
            for index in range(frames)
        ],
        0,
    )
    normed = (layer_norm(embedded) * (1.0 + rows_of[1:2]) + rows_of[0:1]).astype(BF16)
    mixed = attention(normed, input_weight[...], output_weight[...], spatial, None)
    after = embedded + rows_of[2:3] * mixed
    for index in range(frames):
        out[at + index] = after[index * spatial : (index + 1) * spatial].astype(out.dtype)


def time_step(at, count, after, rows_of, input_weight, output_weight, final, out, same_position):
    frames, width = after.shape[0], after.shape[2]
    hidden = jnp.concatenate(
        [
            after[:, pl.ds(pl.multiple_of(at + index * ROWS8, ROWS8), ROWS8), :].reshape(
                frames * ROWS8, width
            )
            for index in range(count)
        ],
        0,
    ).astype(F32)
    normed = (layer_norm(hidden) * (1.0 + rows_of[4:5]) + rows_of[3:4]).astype(BF16)
    mixed = attention(
        normed, input_weight[...], output_weight[...], frames * ROWS8, same_position
    )
    settled = hidden + rows_of[5:6] * mixed
    normed = (layer_norm(settled) * (1.0 + rows_of[7:8]) + rows_of[6:7]).astype(BF16)
    predicted = lax.dot_general(
        normed, final[...], (((1,), (1,)), ((), ())), preferred_element_type=F32
    )
    for index in range(count):
        part = predicted[index * frames * ROWS8 : (index + 1) * frames * ROWS8]
        out[:, pl.ds(pl.multiple_of(at + index * ROWS8, ROWS8), ROWS8), :] = part.reshape(
            frames, ROWS8, part.shape[1]
        )


def same_position_mask(frames):
    rows = frames * ROWS8
    row = lax.broadcasted_iota(jnp.int32, (rows, rows), 0) % ROWS8
    column = lax.broadcasted_iota(jnp.int32, (rows, rows), 1) % ROWS8
    return jnp.where(row == column, 1.0, 0.0).astype(BF16)


def both(blocks):
    return 2 if blocks % 2 == 0 else 1


def run_space(latent, embed, rows_of, input_weight, output_weight, out):
    frames = latent.shape[0]
    step = both(frames)

    @pl.loop(0, frames // step)
    def _(index):
        space_step(index * step, step, latent, embed, rows_of, input_weight, output_weight, out)


def run_time(after, rows_of, input_weight, output_weight, final, out):
    frames, positions = after.shape[0], after.shape[1]
    step = both(positions // ROWS8)
    same_position = same_position_mask(frames)

    @pl.loop(0, positions // (step * ROWS8))
    def _(index):
        time_step(
            index * step * ROWS8, step, after, rows_of, input_weight, output_weight, final, out,
            same_position,
        )


def fused_kernel(
    timestep, rate_state, rate_denoise, rate_noise, latent, noise, modulation, embed,
    space_in_hbm, space_out_hbm, time_in_hbm, time_out_hbm, final, increment, rounded,
    rows_of, space_in, space_out, time_in, time_out, after, staged, sems,
):
    own = timestep[0]
    copies = [
        pltpu.make_async_copy(source, target, sems.at[index])
        for index, (source, target) in enumerate(
            (
                (modulation.at[own], rows_of),
                (space_in_hbm, space_in),
                (space_out_hbm, space_out),
                (time_in_hbm, time_in),
                (time_out_hbm, time_out),
            )
        )
    ]
    for copy in copies:
        copy.start()
    for copy in copies[:3]:
        copy.wait()
    run_space(latent, embed, rows_of, space_in, space_out, after)
    for copy in copies[3:]:
        copy.wait()
    run_time(after, rows_of, time_in, time_out, final, staged)
    keep = rate_state[own] + jnp.where(own == 0, 1.0, 0.0)
    for frame in range(latent.shape[0]):
        value = (
            keep * latent[frame]
            + rate_denoise[own] * staged[frame].T
            + rate_noise[own] * noise[frame]
        )
        increment[frame] = value
        rounded[frame] = value.astype(BF16)


def space_kernel(latent, rows_of, embed, space_in, space_out, after):
    run_space(latent, embed, rows_of, space_in, space_out, after)


def time_kernel(after, rows_of, time_in, time_out, final, predicted):
    run_time(after, rows_of, time_in, time_out, final, predicted)


def vmem(count):
    return [pl.BlockSpec(memory_space=pltpu.VMEM)] * count


PARAMS = dict(compiler_params=pltpu.CompilerParams(vmem_limit_bytes=56 * 2**20))


def scalars(count):
    return [pl.BlockSpec(memory_space=pltpu.SMEM)] * count


def step_fused(timestep, rates, latent, noise, modulation, weights):
    frames, channels, spatial = latent.shape
    embed, space_in, space_out, time_in, time_out, final = weights
    width = embed.shape[1]
    return pl.pallas_call(
        fused_kernel,
        out_shape=[
            jax.ShapeDtypeStruct(latent.shape, F32),
            jax.ShapeDtypeStruct(latent.shape, BF16),
        ],
        in_specs=scalars(4)
        + vmem(2)
        + [pl.BlockSpec(memory_space=pl.ANY)]
        + vmem(1)
        + [pl.BlockSpec(memory_space=pl.ANY)] * 4
        + vmem(1),
        out_specs=vmem(2),
        scratch_shapes=[
            pltpu.VMEM(modulation.shape[1:], F32),
            pltpu.VMEM(space_in.shape, BF16),
            pltpu.VMEM(space_out.shape, BF16),
            pltpu.VMEM(time_in.shape, BF16),
            pltpu.VMEM(time_out.shape, BF16),
            pltpu.VMEM((frames, spatial, width), F32),
            pltpu.VMEM((frames, spatial, channels), F32),
            pltpu.SemaphoreType.DMA((5,)),
        ],
        name="denoise",
        **PARAMS,
    )(
        timestep, *rates, latent, noise, modulation, embed, space_in, space_out, time_in,
        time_out, final,
    )


def step_split(timestep, rates, latent, noise, modulation, weights, peers):
    frames, channels, spatial = latent.shape
    embed, space_in, space_out, time_in, time_out, final = weights
    width = embed.shape[1]
    own = timestep[0]
    rows_of = lax.dynamic_index_in_dim(modulation, own, 0, keepdims=False)
    after = pl.pallas_call(
        space_kernel,
        out_shape=jax.ShapeDtypeStruct((frames, spatial, width), BF16),
        in_specs=vmem(5),
        out_specs=vmem(1)[0],
        name="space",
        **PARAMS,
    )(latent, rows_of, embed, space_in, space_out)
    after = lax.all_to_all(
        after, "tok", split_axis=1, concat_axis=0, tiled=True, axis_index_groups=peers
    )
    predicted = pl.pallas_call(
        time_kernel,
        out_shape=jax.ShapeDtypeStruct(after.shape[:2] + (channels,), F32),
        in_specs=vmem(5),
        out_specs=vmem(1)[0],
        name="time",
        **PARAMS,
    )(after.astype(F32), rows_of, time_in, time_out, final)
    predicted = lax.all_to_all(
        predicted, "tok", split_axis=0, concat_axis=1, tiled=True, axis_index_groups=peers
    )
    rate_state, rate_denoise, rate_noise = (rate[own] for rate in rates)
    increment = (
        (rate_state + jnp.where(own == 0, 1.0, 0.0)) * latent
        + rate_denoise * jnp.swapaxes(predicted, 1, 2)
        + rate_noise * noise
    )
    return increment, increment.astype(BF16)


RADIX = 4


def sum_before(values, held, timesteps, groups):
    before = jnp.zeros_like(values)
    reach = 1
    while reach < timesteps:
        arrived = []
        for back in range(reach, min(reach * RADIX, timesteps), reach):
            moves = [
                (step * groups + block, (step + back) * groups + block)
                for step in range(timesteps - back)
                for block in range(groups)
            ]
            arrived.append(lax.ppermute(held, "tok", moves))
        for part in arrived:
            before = before + part.astype(F32)
        held = (values + before).astype(BF16)
        reach *= RADIX
    return before


def body(
    initial_guess,
    noise_draws,
    drift_state,
    drift_denoise,
    noise_scale,
    modulation,
    embed_weight,
    space_input,
    space_output,
    time_input,
    time_output,
    final_weight,
):
    timesteps = modulation.shape[0]
    devices = lax.axis_size("tok")
    groups = devices // timesteps
    timestep = lax.axis_index("tok") // groups
    leading = timestep == 0
    own = timestep.astype(jnp.int32).reshape(1)
    if groups == 1:
        step = step_fused
    else:
        peers = [[row * groups + block for block in range(groups)] for row in range(timesteps)]
        step = functools.partial(step_split, peers=peers)
    rates = (drift_state, drift_denoise, noise_scale)
    weights = (
        embed_weight, space_input.T, space_output, time_input.T, time_output, final_weight.T
    )
    latent = initial_guess
    result = initial_guess
    for _ in range(ITERS):
        increment, rounded = step(own, rates, latent, noise_draws, modulation, weights)
        before = sum_before(increment, rounded, timesteps, groups)
        result = before + increment
        latent = jnp.where(leading, latent, before)
    return result


def solution(mesh):
    rows = P(("group", "tok"), None, None)
    placed = (rows, rows) + (P(),) * 10
    return jax.shard_map(
        body, mesh=mesh, in_specs=placed, out_specs=rows, check_vma=False
    )
```

```python
import functools
import math

import jax
import jax.numpy as jnp
from jax import lax
from jax.experimental import pallas as pl
from jax.experimental.pallas import tpu as pltpu
from jax.sharding import PartitionSpec as P

HEADS = 8
ITERS = 2
ROWS8 = 8
ROWS16 = 16
F32 = jnp.float32
BF16 = jnp.bfloat16


def layer_norm(values):
    center = values - jnp.mean(values, -1, keepdims=True)
    return center * lax.rsqrt(jnp.mean(center * center, -1, keepdims=True) + 1e-06)


def normed_head(values, head_size, scale):
    total = jnp.sum(values * values, 0, keepdims=True)
    return values * (lax.rsqrt(total * (1.0 / head_size) + 1e-06) * scale)


def padded(values, fill):
    rows, columns = values.shape
    extra = ROWS16 - rows % ROWS16
    return jnp.concatenate([values, jnp.full((extra, columns), fill, F32)], 0).astype(BF16)


def attention(normed, input_turned, output_weight, group_rows, same_position, turned):
    tokens = normed.shape[0]
    inner = output_weight.shape[0]
    head_size = inner // HEADS
    turned_normed, turned_keys, turned_attended = turned
    turned_normed[...] = normed.T
    packed = jnp.dot(input_turned, turned_normed[...], preferred_element_type=F32)
    starts = range(0, tokens, group_rows)
    attended = [[] for _ in starts]
    for head in range(HEADS):
        at = head * head_size
        query = packed[at : at + head_size]
        key = packed[inner + at : inner + at + head_size]
        value = packed[2 * inner + at : 2 * inner + at + head_size]
        query = padded(
            normed_head(query, head_size, head_size ** (-0.5) * math.log2(math.e)), 0.0
        )
        turned_keys[head] = padded(normed_head(key, head_size, 1.0), 0.0).T
        value = padded(value, 1.0)
        for group, start in enumerate(starts):
            columns = slice(start, start + group_rows)
            scores = jnp.dot(
                turned_keys[head, columns], query[:, columns], preferred_element_type=F32
            )
            weights = jnp.exp2(scores).astype(BF16)
            if same_position is not None:
                weights = weights * same_position
            mixed = jnp.dot(value[:, columns], weights, preferred_element_type=F32)
            rate = 1.0 / mixed[head_size : head_size + ROWS8]
            parts = mixed[:head_size].reshape(head_size // ROWS8, ROWS8, group_rows) * rate[None]
            attended[group].append(parts.reshape(head_size, group_rows))
    attended = jnp.concatenate([jnp.concatenate(part, 0) for part in attended], 1).astype(BF16)
    turned_attended[...] = attended.T
    return jnp.dot(turned_attended[...], output_weight, preferred_element_type=F32)


def space_step(at, frames, latent, embed, rows_of, input_weight, output_weight, out, turned):
    spatial = latent.shape[2]
    embedded = jnp.concatenate(
        [
            lax.dot_general(
                latent[at + index].astype(BF16),
                embed[...],
                (((0,), (0,)), ((), ())),
                preferred_element_type=F32,
            )
            for index in range(frames)
        ],
        0,
    )
    normed = (layer_norm(embedded) * (1.0 + rows_of[1:2]) + rows_of[0:1]).astype(BF16)
    mixed = attention(normed, input_weight[...], output_weight[...], spatial, None, turned)
    after = embedded + rows_of[2:3] * mixed
    for index in range(frames):
        out[at + index] = after[index * spatial : (index + 1) * spatial].astype(out.dtype)


def time_step(
    at, count, after, rows_of, input_weight, output_weight, final, out, same_position, turned
):
    frames, width = after.shape[0], after.shape[2]
    hidden = jnp.concatenate(
        [
            after[:, pl.ds(pl.multiple_of(at + index * ROWS8, ROWS8), ROWS8), :].reshape(
                frames * ROWS8, width
            )
            for index in range(count)
        ],
        0,
    ).astype(F32)
    normed = (layer_norm(hidden) * (1.0 + rows_of[4:5]) + rows_of[3:4]).astype(BF16)
    mixed = attention(
        normed, input_weight[...], output_weight[...], frames * ROWS8, same_position, turned
    )
    settled = hidden + rows_of[5:6] * mixed
    normed = (layer_norm(settled) * (1.0 + rows_of[7:8]) + rows_of[6:7]).astype(BF16)
    predicted = lax.dot_general(
        normed, final[...], (((1,), (1,)), ((), ())), preferred_element_type=F32
    )
    for index in range(count):
        part = predicted[index * frames * ROWS8 : (index + 1) * frames * ROWS8]
        out[:, pl.ds(pl.multiple_of(at + index * ROWS8, ROWS8), ROWS8), :] = part.reshape(
            frames, ROWS8, part.shape[1]
        )


def same_position_mask(frames):
    rows = frames * ROWS8
    row = lax.broadcasted_iota(jnp.int32, (rows, rows), 0) % ROWS8
    column = lax.broadcasted_iota(jnp.int32, (rows, rows), 1) % ROWS8
    return jnp.where(row == column, 1.0, 0.0).astype(BF16)


def both(blocks):
    return 2 if blocks % 2 == 0 else 1


def run_space(latent, embed, rows_of, input_weight, output_weight, out, turned):
    frames = latent.shape[0]
    step = both(frames)

    @pl.loop(0, frames // step)
    def _(index):
        space_step(
            index * step, step, latent, embed, rows_of, input_weight, output_weight, out, turned
        )


def run_time(after, rows_of, input_weight, output_weight, final, out, turned):
    frames, positions = after.shape[0], after.shape[1]
    step = both(positions // ROWS8)
    same_position = same_position_mask(frames)

    @pl.loop(0, positions // (step * ROWS8))
    def _(index):
        time_step(
            index * step * ROWS8, step, after, rows_of, input_weight, output_weight, final, out,
            same_position, turned,
        )


def fused_kernel(
    timestep, rate_state, rate_denoise, rate_noise, latent, noise, modulation, embed,
    space_in_hbm, space_out_hbm, time_in_hbm, time_out_hbm, final, increment, rounded,
    rows_of, space_in, space_out, time_in, time_out, after, staged, sems, *turned,
):
    own = timestep[0]
    copies = [
        pltpu.make_async_copy(source, target, sems.at[index])
        for index, (source, target) in enumerate(
            (
                (modulation.at[own], rows_of),
                (space_in_hbm, space_in),
                (space_out_hbm, space_out),
                (time_in_hbm, time_in),
                (time_out_hbm, time_out),
            )
        )
    ]
    for copy in copies:
        copy.start()
    for copy in copies[:3]:
        copy.wait()
    run_space(latent, embed, rows_of, space_in, space_out, after, turned)
    for copy in copies[3:]:
        copy.wait()
    run_time(after, rows_of, time_in, time_out, final, staged, turned)
    keep = rate_state[own] + jnp.where(own == 0, 1.0, 0.0)
    for frame in range(latent.shape[0]):
        value = (
            keep * latent[frame]
            + rate_denoise[own] * staged[frame].T
            + rate_noise[own] * noise[frame]
        )
        increment[frame] = value
        rounded[frame] = value.astype(BF16)


def space_kernel(latent, rows_of, embed, space_in, space_out, after, *turned):
    run_space(latent, embed, rows_of, space_in, space_out, after, turned)


def time_kernel(after, rows_of, time_in, time_out, final, predicted, *turned):
    run_time(after, rows_of, time_in, time_out, final, predicted, turned)


def vmem(count):
    return [pl.BlockSpec(memory_space=pltpu.VMEM)] * count


PARAMS = dict(compiler_params=pltpu.CompilerParams(vmem_limit_bytes=56 * 2**20))


def turned_scratch(tokens, width, inner):
    head_size = inner // HEADS
    return [
        pltpu.VMEM((width, tokens), BF16),
        pltpu.VMEM((HEADS, tokens, head_size + ROWS16 - head_size % ROWS16), BF16),
        pltpu.VMEM((tokens, inner), BF16),
    ]


def scalars(count):
    return [pl.BlockSpec(memory_space=pltpu.SMEM)] * count


def step_fused(timestep, rates, latent, noise, modulation, weights):
    frames, channels, spatial = latent.shape
    embed, space_in, space_out, time_in, time_out, final = weights
    width = embed.shape[1]
    return pl.pallas_call(
        fused_kernel,
        out_shape=[
            jax.ShapeDtypeStruct(latent.shape, F32),
            jax.ShapeDtypeStruct(latent.shape, BF16),
        ],
        in_specs=scalars(4)
        + vmem(2)
        + [pl.BlockSpec(memory_space=pl.ANY)]
        + vmem(1)
        + [pl.BlockSpec(memory_space=pl.ANY)] * 4
        + vmem(1),
        out_specs=vmem(2),
        scratch_shapes=[
            pltpu.VMEM(modulation.shape[1:], F32),
            pltpu.VMEM(space_in.shape, BF16),
            pltpu.VMEM(space_out.shape, BF16),
            pltpu.VMEM(time_in.shape, BF16),
            pltpu.VMEM(time_out.shape, BF16),
            pltpu.VMEM((frames, spatial, width), F32),
            pltpu.VMEM((frames, spatial, channels), F32),
            pltpu.SemaphoreType.DMA((5,)),
        ]
        + turned_scratch(both(frames) * spatial, width, space_out.shape[0]),
        name="denoise",
        **PARAMS,
    )(
        timestep, *rates, latent, noise, modulation, embed, space_in, space_out, time_in,
        time_out, final,
    )


def step_split(timestep, rates, latent, noise, modulation, weights, peers):
    frames, channels, spatial = latent.shape
    embed, space_in, space_out, time_in, time_out, final = weights
    width = embed.shape[1]
    own = timestep[0]
    rows_of = lax.dynamic_index_in_dim(modulation, own, 0, keepdims=False)
    after = pl.pallas_call(
        space_kernel,
        out_shape=jax.ShapeDtypeStruct((frames, spatial, width), BF16),
        in_specs=vmem(5),
        out_specs=vmem(1)[0],
        scratch_shapes=turned_scratch(both(frames) * spatial, width, space_out.shape[0]),
        name="space",
        **PARAMS,
    )(latent, rows_of, embed, space_in, space_out)
    after = lax.all_to_all(
        after, "tok", split_axis=1, concat_axis=0, tiled=True, axis_index_groups=peers
    )
    predicted = pl.pallas_call(
        time_kernel,
        out_shape=jax.ShapeDtypeStruct(after.shape[:2] + (channels,), F32),
        in_specs=vmem(5),
        out_specs=vmem(1)[0],
        scratch_shapes=turned_scratch(
            both(after.shape[1] // ROWS8) * ROWS8 * after.shape[0], width, time_out.shape[0]
        ),
        name="time",
        **PARAMS,
    )(after.astype(F32), rows_of, time_in, time_out, final)
    predicted = lax.all_to_all(
        predicted, "tok", split_axis=0, concat_axis=1, tiled=True, axis_index_groups=peers
    )
    rate_state, rate_denoise, rate_noise = (rate[own] for rate in rates)
    increment = (
        (rate_state + jnp.where(own == 0, 1.0, 0.0)) * latent
        + rate_denoise * jnp.swapaxes(predicted, 1, 2)
        + rate_noise * noise
    )
    return increment, increment.astype(BF16)


RADIX = 4


def sum_before(values, held, timesteps, groups):
    before = jnp.zeros_like(values)
    reach = 1
    while reach < timesteps:
        arrived = []
        for back in range(reach, min(reach * RADIX, timesteps), reach):
            moves = [
                (step * groups + block, (step + back) * groups + block)
                for step in range(timesteps - back)
                for block in range(groups)
            ]
            arrived.append(lax.ppermute(held, "tok", moves))
        for part in arrived:
            before = before + part.astype(F32)
        held = (values + before).astype(BF16)
        reach *= RADIX
    return before


def body(
    initial_guess,
    noise_draws,
    drift_state,
    drift_denoise,
    noise_scale,
    modulation,
    embed_weight,
    space_input,
    space_output,
    time_input,
    time_output,
    final_weight,
):
    timesteps = modulation.shape[0]
    devices = lax.axis_size("tok")
    groups = devices // timesteps
    timestep = lax.axis_index("tok") // groups
    leading = timestep == 0
    own = timestep.astype(jnp.int32).reshape(1)
    if groups == 1:
        step = step_fused
    else:
        peers = [[row * groups + block for block in range(groups)] for row in range(timesteps)]
        step = functools.partial(step_split, peers=peers)
    rates = (drift_state, drift_denoise, noise_scale)
    weights = (
        embed_weight, space_input.T, space_output, time_input.T, time_output, final_weight.T
    )
    latent = initial_guess
    result = initial_guess
    for _ in range(ITERS):
        increment, rounded = step(own, rates, latent, noise_draws, modulation, weights)
        before = sum_before(increment, rounded, timesteps, groups)
        result = before + increment
        latent = jnp.where(leading, latent, before)
    return result


def solution(mesh):
    rows = P(("group", "tok"), None, None)
    placed = (rows, rows) + (P(),) * 10
    return jax.shard_map(
        body, mesh=mesh, in_specs=placed, out_specs=rows, check_vma=False
    )
```

```python
import functools
import math

import jax
import jax.numpy as jnp
from jax import lax
from jax.experimental import pallas as pl
from jax.experimental.pallas import tpu as pltpu
from jax.sharding import PartitionSpec as P

HEADS = 8
ITERS = 2
LANES = 128
ROWS8 = 8
ROWS16 = 16
F32 = jnp.float32
BF16 = jnp.bfloat16


def layer_norm(values):
    center = values - jnp.mean(values, -1, keepdims=True)
    return center * lax.rsqrt(jnp.mean(center * center, -1, keepdims=True) + 1e-06)


def normed_head(values, head_size, scale):
    total = jnp.sum(values * values, 0, keepdims=True)
    return values * (lax.rsqrt(total * (1.0 / head_size) + 1e-06) * scale)


def padded(values, fill, rows):
    extra = rows - values.shape[0]
    return jnp.concatenate(
        [values, jnp.full((extra, values.shape[1]), fill, F32)], 0
    ).astype(BF16)


def on_diagonal(blocks):
    zero = jnp.zeros_like(blocks[0])
    return jnp.concatenate(
        [
            jnp.concatenate([block if at == own else zero for at in range(len(blocks))], 1)
            for own, block in enumerate(blocks)
        ],
        0,
    )


def attention(normed, input_turned, output_weight, group_rows, same_position, places):
    turned_normed, query_rows, turned_keys, value_rows, kept, turned_attended = places
    tokens = normed.shape[0]
    inner = output_weight.shape[0]
    head_size = inner // HEADS
    deep, tall = query_rows.shape[1], value_rows.shape[1]
    groups = [slice(at, at + group_rows) for at in range(0, tokens, group_rows)]
    turned_normed[...] = normed.T
    chunk = HEADS // 2
    for kind in range(3):
        for first in range(0, HEADS, chunk):
            at = kind * inner + first * head_size
            packed = jnp.dot(
                input_turned[at : at + chunk * head_size],
                turned_normed[...],
                preferred_element_type=F32,
            )
            for index in range(chunk):
                head = first + index
                values = packed[index * head_size : (index + 1) * head_size]
                if kind == 0:
                    scale = head_size ** (-0.5) * math.log2(math.e)
                    query_rows[head] = padded(normed_head(values, head_size, scale), 0.0, deep)
                elif kind == 1:
                    turned_keys[head] = padded(normed_head(values, head_size, 1.0), 0.0, deep).T
                else:
                    value_rows[head] = padded(values, 1.0, tall)

    def scores_of(head):
        return jnp.dot(
            jnp.concatenate([turned_keys[head, group] for group in groups], 1),
            on_diagonal([query_rows[head, :, group] for group in groups]),
            preferred_element_type=F32,
        )

    ahead = scores_of(0)
    for head in range(HEADS):
        scores, ahead = ahead, scores_of(head + 1) if head + 1 < HEADS else None
        weights = jnp.exp2(scores).astype(BF16)
        if same_position is not None:
            weights = weights * same_position
        kept[head] = weights

    def mixed_of(head):
        weights = kept[head]
        return jnp.dot(
            value_rows[head],
            on_diagonal([weights[:, group] for group in groups]),
            preferred_element_type=F32,
        )

    attended = []
    ahead = mixed_of(0)
    for head in range(HEADS):
        mixed, ahead = ahead, mixed_of(head + 1) if head + 1 < HEADS else None
        rate = 1.0 / mixed[head_size : head_size + ROWS8]
        parts = mixed[:head_size].reshape(head_size // ROWS8, ROWS8, tokens) * rate[None]
        attended.append(parts.reshape(head_size, tokens))
    turned_attended[...] = jnp.concatenate(attended, 0).astype(BF16).T
    return jnp.dot(turned_attended[...], output_weight[...], preferred_element_type=F32)


def space_step(at, frames, latent, embed, rows_of, input_weight, output_weight, out, turned):
    spatial = latent.shape[2]
    embedded = jnp.concatenate(
        [
            lax.dot_general(
                latent[at + index].astype(BF16),
                embed[...],
                (((0,), (0,)), ((), ())),
                preferred_element_type=F32,
            )
            for index in range(frames)
        ],
        0,
    )
    normed = (layer_norm(embedded) * (1.0 + rows_of[1:2]) + rows_of[0:1]).astype(BF16)
    mixed = attention(normed, input_weight, output_weight, spatial, None, turned)
    after = embedded + rows_of[2:3] * mixed
    for index in range(frames):
        out[at + index] = after[index * spatial : (index + 1) * spatial].astype(out.dtype)


def time_step(
    at, count, after, rows_of, input_weight, output_weight, final, out, same_position, turned
):
    frames, width = after.shape[0], after.shape[2]
    hidden = jnp.concatenate(
        [
            after[:, pl.ds(pl.multiple_of(at + index * ROWS8, ROWS8), ROWS8), :].reshape(
                frames * ROWS8, width
            )
            for index in range(count)
        ],
        0,
    ).astype(F32)
    normed = (layer_norm(hidden) * (1.0 + rows_of[4:5]) + rows_of[3:4]).astype(BF16)
    mixed = attention(
        normed, input_weight, output_weight, frames * ROWS8, same_position, turned
    )
    settled = hidden + rows_of[5:6] * mixed
    normed = (layer_norm(settled) * (1.0 + rows_of[7:8]) + rows_of[6:7]).astype(BF16)
    predicted = lax.dot_general(
        normed, final[...], (((1,), (1,)), ((), ())), preferred_element_type=F32
    )
    for index in range(count):
        part = predicted[index * frames * ROWS8 : (index + 1) * frames * ROWS8]
        out[:, pl.ds(pl.multiple_of(at + index * ROWS8, ROWS8), ROWS8), :] = part.reshape(
            frames, ROWS8, part.shape[1]
        )


def same_position_mask(frames, count):
    shape = (frames * ROWS8, count * frames * ROWS8)
    row = lax.broadcasted_iota(jnp.int32, shape, 0) % ROWS8
    column = lax.broadcasted_iota(jnp.int32, shape, 1) % ROWS8
    return jnp.where(row == column, 1.0, 0.0).astype(BF16)


def both(blocks):
    return 2 if blocks % 2 == 0 else 1


def run_space(latent, embed, rows_of, input_weight, output_weight, out, turned):
    frames = latent.shape[0]
    step = both(frames)

    @pl.loop(0, frames // step)
    def _(index):
        space_step(
            index * step, step, latent, embed, rows_of, input_weight, output_weight, out, turned
        )


def run_time(after, rows_of, input_weight, output_weight, final, out, turned):
    frames, positions = after.shape[0], after.shape[1]
    step = both(positions // ROWS8)
    same_position = same_position_mask(frames, step)

    @pl.loop(0, positions // (step * ROWS8))
    def _(index):
        time_step(
            index * step * ROWS8, step, after, rows_of, input_weight, output_weight, final, out,
            same_position, turned,
        )


def fused_kernel(
    timestep, rate_state, rate_denoise, rate_noise, latent, noise, modulation, embed,
    space_in_hbm, space_out_hbm, time_in_hbm, time_out_hbm, final, increment, rounded,
    rows_of, space_in, space_out, time_in, time_out, after, staged, sems, *turned,
):
    own = timestep[0]
    copies = [
        pltpu.make_async_copy(source, target, sems.at[index])
        for index, (source, target) in enumerate(
            (
                (modulation.at[own], rows_of),
                (space_in_hbm, space_in),
                (space_out_hbm, space_out),
                (time_in_hbm, time_in),
                (time_out_hbm, time_out),
            )
        )
    ]
    for copy in copies:
        copy.start()
    for copy in copies[:3]:
        copy.wait()
    run_space(latent, embed, rows_of, space_in, space_out, after, turned)
    for copy in copies[3:]:
        copy.wait()
    run_time(after, rows_of, time_in, time_out, final, staged, turned)
    keep = rate_state[own] + jnp.where(own == 0, 1.0, 0.0)
    for frame in range(latent.shape[0]):
        value = (
            keep * latent[frame]
            + rate_denoise[own] * staged[frame].T
            + rate_noise[own] * noise[frame]
        )
        increment[frame] = value
        rounded[frame] = value.astype(BF16)


def space_kernel(latent, rows_of, embed, space_in, space_out, after, *turned):
    run_space(latent, embed, rows_of, space_in, space_out, after, turned)


def time_kernel(after, rows_of, time_in, time_out, final, predicted, *turned):
    run_time(after, rows_of, time_in, time_out, final, predicted, turned)


def vmem(count):
    return [pl.BlockSpec(memory_space=pltpu.VMEM)] * count


PARAMS = dict(compiler_params=pltpu.CompilerParams(vmem_limit_bytes=56 * 2**20))


def turned_scratch(tokens, group_rows, width, inner):
    head_size = inner // HEADS
    deep = -(-head_size // LANES) * LANES
    tall = head_size + ROWS16 - head_size % ROWS16
    return [
        pltpu.VMEM((width, tokens), BF16),
        pltpu.VMEM((HEADS, deep, tokens), BF16),
        pltpu.VMEM((HEADS, tokens, deep), BF16),
        pltpu.VMEM((HEADS, tall, tokens), BF16),
        pltpu.VMEM((HEADS, group_rows, tokens), BF16),
        pltpu.VMEM((tokens, inner), BF16),
    ]


def scalars(count):
    return [pl.BlockSpec(memory_space=pltpu.SMEM)] * count


def step_fused(timestep, rates, latent, noise, modulation, weights):
    frames, channels, spatial = latent.shape
    embed, space_in, space_out, time_in, time_out, final = weights
    width = embed.shape[1]
    return pl.pallas_call(
        fused_kernel,
        out_shape=[
            jax.ShapeDtypeStruct(latent.shape, F32),
            jax.ShapeDtypeStruct(latent.shape, BF16),
        ],
        in_specs=scalars(4)
        + vmem(2)
        + [pl.BlockSpec(memory_space=pl.ANY)]
        + vmem(1)
        + [pl.BlockSpec(memory_space=pl.ANY)] * 4
        + vmem(1),
        out_specs=vmem(2),
        scratch_shapes=[
            pltpu.VMEM(modulation.shape[1:], F32),
            pltpu.VMEM(space_in.shape, BF16),
            pltpu.VMEM(space_out.shape, BF16),
            pltpu.VMEM(time_in.shape, BF16),
            pltpu.VMEM(time_out.shape, BF16),
            pltpu.VMEM((frames, spatial, width), F32),
            pltpu.VMEM((frames, spatial, channels), F32),
            pltpu.SemaphoreType.DMA((5,)),
        ]
        + turned_scratch(both(frames) * spatial, spatial, width, space_out.shape[0]),
        name="denoise",
        **PARAMS,
    )(
        timestep, *rates, latent, noise, modulation, embed, space_in, space_out, time_in,
        time_out, final,
    )


def step_split(timestep, rates, latent, noise, modulation, weights, peers):
    frames, channels, spatial = latent.shape
    embed, space_in, space_out, time_in, time_out, final = weights
    width = embed.shape[1]
    own = timestep[0]
    rows_of = lax.dynamic_index_in_dim(modulation, own, 0, keepdims=False)
    after = pl.pallas_call(
        space_kernel,
        out_shape=jax.ShapeDtypeStruct((frames, spatial, width), BF16),
        in_specs=vmem(5),
        out_specs=vmem(1)[0],
        scratch_shapes=turned_scratch(both(frames) * spatial, spatial, width, space_out.shape[0]),
        name="space",
        **PARAMS,
    )(latent, rows_of, embed, space_in, space_out)
    after = lax.all_to_all(
        after, "tok", split_axis=1, concat_axis=0, tiled=True, axis_index_groups=peers
    )
    predicted = pl.pallas_call(
        time_kernel,
        out_shape=jax.ShapeDtypeStruct(after.shape[:2] + (channels,), F32),
        in_specs=vmem(5),
        out_specs=vmem(1)[0],
        scratch_shapes=turned_scratch(
            both(after.shape[1] // ROWS8) * ROWS8 * after.shape[0], ROWS8 * after.shape[0],
            width, time_out.shape[0],
        ),
        name="time",
        **PARAMS,
    )(after.astype(F32), rows_of, time_in, time_out, final)
    predicted = lax.all_to_all(
        predicted, "tok", split_axis=0, concat_axis=1, tiled=True, axis_index_groups=peers
    )
    rate_state, rate_denoise, rate_noise = (rate[own] for rate in rates)
    increment = (
        (rate_state + jnp.where(own == 0, 1.0, 0.0)) * latent
        + rate_denoise * jnp.swapaxes(predicted, 1, 2)
        + rate_noise * noise
    )
    return increment, increment.astype(BF16)


RADIX = 4


def sum_before(values, held, timesteps, groups):
    before = jnp.zeros_like(values)
    reach = 1
    while reach < timesteps:
        arrived = []
        for back in range(reach, min(reach * RADIX, timesteps), reach):
            moves = [
                (step * groups + block, (step + back) * groups + block)
                for step in range(timesteps - back)
                for block in range(groups)
            ]
            arrived.append(lax.ppermute(held, "tok", moves))
        for part in arrived:
            before = before + part.astype(F32)
        held = (values + before).astype(BF16)
        reach *= RADIX
    return before


def body(
    initial_guess,
    noise_draws,
    drift_state,
    drift_denoise,
    noise_scale,
    modulation,
    embed_weight,
    space_input,
    space_output,
    time_input,
    time_output,
    final_weight,
):
    timesteps = modulation.shape[0]
    devices = lax.axis_size("tok")
    groups = devices // timesteps
    timestep = lax.axis_index("tok") // groups
    leading = timestep == 0
    own = timestep.astype(jnp.int32).reshape(1)
    if groups == 1:
        step = step_fused
    else:
        peers = [[row * groups + block for block in range(groups)] for row in range(timesteps)]
        step = functools.partial(step_split, peers=peers)
    rates = (drift_state, drift_denoise, noise_scale)
    weights = (
        embed_weight, space_input.T, space_output, time_input.T, time_output, final_weight.T
    )
    latent = initial_guess
    result = initial_guess
    for _ in range(ITERS):
        increment, rounded = step(own, rates, latent, noise_draws, modulation, weights)
        before = sum_before(increment, rounded, timesteps, groups)
        result = before + increment
        latent = jnp.where(leading, latent, before)
    return result


def solution(mesh):
    rows = P(("group", "tok"), None, None)
    placed = (rows, rows) + (P(),) * 10
    return jax.shard_map(
        body, mesh=mesh, in_specs=placed, out_specs=rows, check_vma=False
    )
```

```python
import functools
import itertools
import math

import jax
import jax.numpy as jnp
from jax import lax
from jax.experimental import pallas as pl
from jax.experimental.pallas import tpu as pltpu
from jax.sharding import PartitionSpec as P

HEADS = 8
ITERS = 2
LANES = 128
ROWS8 = 8
ROWS16 = 16
F32 = jnp.float32
BF16 = jnp.bfloat16


def layer_norm(values):
    center = values - jnp.mean(values, -1, keepdims=True)
    return center * lax.rsqrt(jnp.mean(center * center, -1, keepdims=True) + 1e-06)


def normed_head(values, head_size, scale):
    total = jnp.sum(values * values, 0, keepdims=True)
    return values * (lax.rsqrt(total * (1.0 / head_size) + 1e-06) * scale)


def padded(values, fill, rows):
    extra = rows - values.shape[0]
    return jnp.concatenate(
        [values, jnp.full((extra, values.shape[1]), fill, F32)], 0
    ).astype(BF16)


def on_diagonal(blocks):
    zero = jnp.zeros_like(blocks[0])
    return jnp.concatenate(
        [
            jnp.concatenate([block if at == own else zero for at in range(len(blocks))], 1)
            for own, block in enumerate(blocks)
        ],
        0,
    )


def modulated_norm(values, rows_of, shift, scale):
    return (
        layer_norm(values) * (1.0 + rows_of[scale : scale + 1]) + rows_of[shift : shift + 1]
    ).astype(BF16)


def weave(main, side, main_count, side_count):
    done = 0
    for index, _ in enumerate(main):
        due = -(-(index + 1) * side_count // main_count)
        while done < due:
            next(side, None)
            done += 1
    for _ in side:
        pass


def turn(source, target, tokens, width):
    for at in range(0, width, LANES):
        target[at : at + LANES, :] = source[:, at : at + LANES].T
        yield


def attention_pieces(turned_normed, input_turned, output_weight, same_position, places, groups, finish):
    query_rows, turned_keys, value_rows, kept, attended, turned_attended = places
    inner, width = output_weight.shape
    tokens = turned_normed.shape[1]
    head_size = inner // HEADS
    deep, tall = query_rows.shape[1], value_rows.shape[1]
    chunk = HEADS // 2
    scale = head_size ** (-0.5) * math.log2(math.e)

    def project(kind, half):
        at = kind * inner + half * chunk * head_size
        rows = input_turned[at : at + chunk * head_size]
        return jnp.dot(rows, turned_normed[...], preferred_element_type=F32)

    def keep_projected(kind, half, packed):
        for index in range(chunk):
            head = half * chunk + index
            values = packed[index * head_size : (index + 1) * head_size]
            if kind == 0:
                query_rows[head] = padded(normed_head(values, head_size, scale), 0.0, deep)
            elif kind == 1:
                turned_keys[head] = padded(normed_head(values, head_size, 1.0), 0.0, deep).T
            else:
                value_rows[head] = padded(values, 1.0, tall)

    def score(head):
        return jnp.dot(
            jnp.concatenate([turned_keys[head, group] for group in groups], 1),
            on_diagonal([query_rows[head, :, group] for group in groups]),
            preferred_element_type=F32,
        )

    def keep_scored(head, scores):
        weights = jnp.exp2(scores).astype(BF16)
        kept[head] = weights if same_position is None else weights * same_position

    def mix(head):
        return jnp.dot(
            value_rows[head],
            on_diagonal([kept[head, :, group] for group in groups]),
            preferred_element_type=F32,
        )

    def keep_mixed(head, mixed):
        rate = 1.0 / mixed[head_size : head_size + ROWS8]
        parts = mixed[:head_size].reshape(head_size // ROWS8, ROWS8, tokens) * rate[None]
        first, last = head * head_size, (head + 1) * head_size
        attended[first:last] = parts.reshape(head_size, tokens)
        for at in range(0, inner, LANES):
            stop = min(at + LANES, inner)
            if first < stop <= last:
                turned_attended[:, at:stop] = attended[at:stop].astype(BF16).T

    def projections(kind, half):
        return (lambda: project(kind, half)), (lambda got: keep_projected(kind, half, got))

    def scorings(head):
        return (lambda: score(head)), (lambda got: keep_scored(head, got))

    def mixings(head):
        return (lambda: mix(head)), (lambda got: keep_mixed(head, got))

    def outputs(at):
        columns = slice(at, min(at + 2 * LANES, width))
        return (
            lambda: jnp.dot(
                turned_attended[...], output_weight[:, columns], preferred_element_type=F32
            )
        ), (lambda got: finish(columns, got))

    scored = [scorings(head) for head in range(HEADS)]
    mixes = [mixings(head) for head in range(HEADS)]
    first = [projections(0, 0), projections(1, 0), projections(0, 1)]
    for later, task in zip((projections(1, 1), projections(2, 0), projections(2, 1)), scored):
        first += [task, later]
    behind = scored[3:]
    for index, task in enumerate(behind):
        first.append(task)
        if index >= 1:
            first.append(mixes[index - 1])
    first += mixes[len(behind) - 1 :]
    for tasks in (first, [outputs(at) for at in range(0, width, 2 * LANES)]):
        waiting = None
        for issue, use in tasks:
            got = issue()
            if waiting is not None:
                waiting[0](waiting[1])
            waiting = (use, got)
            yield
        waiting[0](waiting[1])
        yield


def run_pipelined(steps, before, main, behind, main_count, before_count, behind_count):
    def one(index, own, last):
        following = jnp.minimum(index + 1, last)
        previous = jnp.maximum(index - 1, 0)
        side = itertools.chain(behind(previous, 1 - own), before(following, 1 - own))
        weave(main(index, own), side, main_count, before_count + behind_count)

    for _ in before(0, 0):
        pass
    if steps % 2 == 0:

        @pl.loop(0, steps // 2)
        def _(turn_index):
            one(2 * turn_index, 0, steps - 1)
            one(2 * turn_index + 1, 1, steps - 1)

        for _ in behind(steps - 1, 1):
            pass
    else:
        for index in range(steps):
            one(index, index % 2, steps - 1)
        for _ in behind(steps - 1, (steps - 1) % 2):
            pass


BLOCK = 32


def run_space(latent, embed, rows_of, input_weight, output_weight, out, places):
    frames, _, spatial = latent.shape
    width = embed.shape[1]
    step = both(frames)
    tokens = step * spatial
    plain, turned, base, inner_places = places[0], places[1:3], places[3:5], places[5:]
    groups = [slice(at, at + spatial) for at in range(0, tokens, spatial)]

    def before(index, own):
        for frame in range(step):
            base[own][groups[frame]] = lax.dot_general(
                latent[index * step + frame].astype(BF16),
                embed[...],
                (((0,), (0,)), ((), ())),
                preferred_element_type=F32,
            )
            yield
        for at in range(0, tokens, BLOCK):
            plain[at : at + BLOCK] = modulated_norm(base[own][at : at + BLOCK], rows_of, 0, 1)
            yield
        yield from turn(plain, turned[own], tokens, width)

    def main(index, own):
        def finish(columns, mixed):
            after = base[own][:, columns] + rows_of[2:3, columns] * mixed
            for frame, group in enumerate(groups):
                out[index * step + frame, :, columns] = after[group].astype(out.dtype)

        return attention_pieces(
            turned[own], input_weight, output_weight, None, inner_places, groups, finish
        )

    def behind(index, own):
        return iter(())

    run_pipelined(
        frames // step, before, main, behind, 29, step + tokens // BLOCK + width // LANES, 0
    )


def run_time(after, rows_of, input_weight, output_weight, final, out, places):
    frames, positions, width = after.shape
    step = both(positions // ROWS8)
    rows = frames * ROWS8
    tokens = step * rows
    plain, turned, settled, inner_places = places[0], places[1:3], places[3:5], places[5:]
    groups = [slice(at, at + rows) for at in range(0, tokens, rows)]
    same_position = same_position_mask(frames, step)

    def eight(index, group):
        at = (index * step + group) * ROWS8
        if not isinstance(at, int):
            at = pl.multiple_of(at, ROWS8)
        return pl.ds(at, ROWS8)

    def before(index, own):
        for group in range(step):
            for at in range(0, rows, BLOCK):
                some = slice(at // ROWS8, (at + BLOCK) // ROWS8)
                hidden = after[some, eight(index, group), :].reshape(BLOCK, width)
                first = groups[group].start + at
                plain[first : first + BLOCK] = modulated_norm(hidden, rows_of, 3, 4)
                yield
        yield from turn(plain, turned[own], tokens, width)

    def main(index, own):
        def finish(columns, mixed):
            for group in range(step):
                hidden = after[:, eight(index, group), columns].reshape(rows, -1)
                settled[own][groups[group], columns] = (
                    hidden + rows_of[5:6, columns] * mixed[groups[group]]
                )

        return attention_pieces(
            turned[own], input_weight, output_weight, same_position, inner_places, groups, finish
        )

    def behind(index, own):
        for group in range(step):
            for at in range(0, rows, BLOCK):
                first = groups[group].start + at
                normed = modulated_norm(settled[own][first : first + BLOCK], rows_of, 6, 7)
                predicted = lax.dot_general(
                    normed, final[...], (((1,), (1,)), ((), ())), preferred_element_type=F32
                )
                some = slice(at // ROWS8, (at + BLOCK) // ROWS8)
                out[some, eight(index, group), :] = predicted.reshape(
                    BLOCK // ROWS8, ROWS8, predicted.shape[1]
                )
                yield

    settled[1][...] = jnp.zeros_like(settled[1])
    run_pipelined(
        positions // (step * ROWS8), before, main, behind, 29,
        tokens // BLOCK + width // LANES, tokens // BLOCK,
    )


def same_position_mask(frames, count):
    shape = (frames * ROWS8, count * frames * ROWS8)
    row = lax.broadcasted_iota(jnp.int32, shape, 0) % ROWS8
    column = lax.broadcasted_iota(jnp.int32, shape, 1) % ROWS8
    return jnp.where(row == column, 1.0, 0.0).astype(BF16)


def both(blocks):
    return 2 if blocks % 2 == 0 else 1


def fused_kernel(
    timestep, rate_state, rate_denoise, rate_noise, latent, noise, modulation, embed,
    space_in_hbm, space_out_hbm, time_in_hbm, time_out_hbm, final, increment, rounded,
    rows_of, space_in, space_out, time_in, time_out, after, staged, sems, *turned,
):
    own = timestep[0]
    copies = [
        pltpu.make_async_copy(source, target, sems.at[index])
        for index, (source, target) in enumerate(
            (
                (modulation.at[own], rows_of),
                (space_in_hbm, space_in),
                (space_out_hbm, space_out),
                (time_in_hbm, time_in),
                (time_out_hbm, time_out),
            )
        )
    ]
    for copy in copies:
        copy.start()
    for copy in copies[:3]:
        copy.wait()
    run_space(latent, embed, rows_of, space_in, space_out, after, turned)
    for copy in copies[3:]:
        copy.wait()
    run_time(after, rows_of, time_in, time_out, final, staged, turned)
    keep = rate_state[own] + jnp.where(own == 0, 1.0, 0.0)
    for frame in range(latent.shape[0]):
        value = (
            keep * latent[frame]
            + rate_denoise[own] * staged[frame].T
            + rate_noise[own] * noise[frame]
        )
        increment[frame] = value
        rounded[frame] = value.astype(BF16)


def space_kernel(latent, rows_of, embed, space_in, space_out, after, *turned):
    run_space(latent, embed, rows_of, space_in, space_out, after, turned)


def time_kernel(after, rows_of, time_in, time_out, final, predicted, *turned):
    run_time(after, rows_of, time_in, time_out, final, predicted, turned)


def vmem(count):
    return [pl.BlockSpec(memory_space=pltpu.VMEM)] * count


PARAMS = dict(compiler_params=pltpu.CompilerParams(vmem_limit_bytes=56 * 2**20))


def turned_scratch(tokens, group_rows, width, inner):
    head_size = inner // HEADS
    deep = -(-head_size // LANES) * LANES
    tall = head_size + ROWS16 - head_size % ROWS16
    return [
        pltpu.VMEM((tokens, width), BF16),
        pltpu.VMEM((width, tokens), BF16),
        pltpu.VMEM((width, tokens), BF16),
        pltpu.VMEM((tokens, width), F32),
        pltpu.VMEM((tokens, width), F32),
        pltpu.VMEM((HEADS, deep, tokens), BF16),
        pltpu.VMEM((HEADS, tokens, deep), BF16),
        pltpu.VMEM((HEADS, tall, tokens), BF16),
        pltpu.VMEM((HEADS, group_rows, tokens), BF16),
        pltpu.VMEM((inner, tokens), F32),
        pltpu.VMEM((tokens, inner), BF16),
    ]


def scalars(count):
    return [pl.BlockSpec(memory_space=pltpu.SMEM)] * count


def step_fused(timestep, rates, latent, noise, modulation, weights):
    frames, channels, spatial = latent.shape
    embed, space_in, space_out, time_in, time_out, final = weights
    width = embed.shape[1]
    return pl.pallas_call(
        fused_kernel,
        out_shape=[
            jax.ShapeDtypeStruct(latent.shape, F32),
            jax.ShapeDtypeStruct(latent.shape, BF16),
        ],
        in_specs=scalars(4)
        + vmem(2)
        + [pl.BlockSpec(memory_space=pl.ANY)]
        + vmem(1)
        + [pl.BlockSpec(memory_space=pl.ANY)] * 4
        + vmem(1),
        out_specs=vmem(2),
        scratch_shapes=[
            pltpu.VMEM(modulation.shape[1:], F32),
            pltpu.VMEM(space_in.shape, BF16),
            pltpu.VMEM(space_out.shape, BF16),
            pltpu.VMEM(time_in.shape, BF16),
            pltpu.VMEM(time_out.shape, BF16),
            pltpu.VMEM((frames, spatial, width), F32),
            pltpu.VMEM((frames, spatial, channels), F32),
            pltpu.SemaphoreType.DMA((5,)),
        ]
        + turned_scratch(both(frames) * spatial, spatial, width, space_out.shape[0]),
        name="denoise",
        **PARAMS,
    )(
        timestep, *rates, latent, noise, modulation, embed, space_in, space_out, time_in,
        time_out, final,
    )


def step_split(timestep, rates, latent, noise, modulation, weights, peers):
    frames, channels, spatial = latent.shape
    embed, space_in, space_out, time_in, time_out, final = weights
    width = embed.shape[1]
    own = timestep[0]
    rows_of = lax.dynamic_index_in_dim(modulation, own, 0, keepdims=False)
    after = pl.pallas_call(
        space_kernel,
        out_shape=jax.ShapeDtypeStruct((frames, spatial, width), BF16),
        in_specs=vmem(5),
        out_specs=vmem(1)[0],
        scratch_shapes=turned_scratch(both(frames) * spatial, spatial, width, space_out.shape[0]),
        name="space",
        **PARAMS,
    )(latent, rows_of, embed, space_in, space_out)
    after = lax.all_to_all(
        after, "tok", split_axis=1, concat_axis=0, tiled=True, axis_index_groups=peers
    )
    predicted = pl.pallas_call(
        time_kernel,
        out_shape=jax.ShapeDtypeStruct(after.shape[:2] + (channels,), F32),
        in_specs=vmem(5),
        out_specs=vmem(1)[0],
        scratch_shapes=turned_scratch(
            both(after.shape[1] // ROWS8) * ROWS8 * after.shape[0], ROWS8 * after.shape[0],
            width, time_out.shape[0],
        ),
        name="time",
        **PARAMS,
    )(after.astype(F32), rows_of, time_in, time_out, final)
    predicted = lax.all_to_all(
        predicted, "tok", split_axis=0, concat_axis=1, tiled=True, axis_index_groups=peers
    )
    rate_state, rate_denoise, rate_noise = (rate[own] for rate in rates)
    increment = (
        (rate_state + jnp.where(own == 0, 1.0, 0.0)) * latent
        + rate_denoise * jnp.swapaxes(predicted, 1, 2)
        + rate_noise * noise
    )
    return increment, increment.astype(BF16)


RADIX = 4


def sum_before(values, held, timesteps, groups):
    before = jnp.zeros_like(values)
    reach = 1
    while reach < timesteps:
        arrived = []
        for back in range(reach, min(reach * RADIX, timesteps), reach):
            moves = [
                (step * groups + block, (step + back) * groups + block)
                for step in range(timesteps - back)
                for block in range(groups)
            ]
            arrived.append(lax.ppermute(held, "tok", moves))
        for part in arrived:
            before = before + part.astype(F32)
        held = (values + before).astype(BF16)
        reach *= RADIX
    return before


def body(
    initial_guess,
    noise_draws,
    drift_state,
    drift_denoise,
    noise_scale,
    modulation,
    embed_weight,
    space_input,
    space_output,
    time_input,
    time_output,
    final_weight,
):
    timesteps = modulation.shape[0]
    devices = lax.axis_size("tok")
    groups = devices // timesteps
    timestep = lax.axis_index("tok") // groups
    leading = timestep == 0
    own = timestep.astype(jnp.int32).reshape(1)
    if groups == 1:
        step = step_fused
    else:
        peers = [[row * groups + block for block in range(groups)] for row in range(timesteps)]
        step = functools.partial(step_split, peers=peers)
    rates = (drift_state, drift_denoise, noise_scale)
    weights = (
        embed_weight, space_input.T, space_output, time_input.T, time_output, final_weight.T
    )
    latent = initial_guess
    result = initial_guess
    for _ in range(ITERS):
        increment, rounded = step(own, rates, latent, noise_draws, modulation, weights)
        before = sum_before(increment, rounded, timesteps, groups)
        result = before + increment
        latent = jnp.where(leading, latent, before)
    return result


def solution(mesh):
    rows = P(("group", "tok"), None, None)
    placed = (rows, rows) + (P(),) * 10
    return jax.shard_map(
        body, mesh=mesh, in_specs=placed, out_specs=rows, check_vma=False
    )
```

```python
import functools
import itertools
import math

import jax
import jax.numpy as jnp
from jax import lax
from jax.experimental import pallas as pl
from jax.experimental.pallas import tpu as pltpu
from jax.sharding import PartitionSpec as P

HEADS = 8
ITERS = 2
LANES = 128
ROWS8 = 8
ROWS16 = 16
F32 = jnp.float32
BF16 = jnp.bfloat16


def layer_norm(values):
    center = values - jnp.mean(values, -1, keepdims=True)
    return center * lax.rsqrt(jnp.mean(center * center, -1, keepdims=True) + 1e-06)


def normed_head(values, head_size, scale):
    total = jnp.sum(values * values, 0, keepdims=True)
    return values * (lax.rsqrt(total * (1.0 / head_size) + 1e-06) * scale)


def padded(values, fill, rows):
    extra = rows - values.shape[0]
    return jnp.concatenate(
        [values, jnp.full((extra, values.shape[1]), fill, F32)], 0
    ).astype(BF16)


def on_diagonal(blocks):
    zero = jnp.zeros_like(blocks[0])
    return jnp.concatenate(
        [
            jnp.concatenate([block if at == own else zero for at in range(len(blocks))], 1)
            for own, block in enumerate(blocks)
        ],
        0,
    )


def modulated_norm(values, rows_of, shift, scale):
    return (
        layer_norm(values) * (1.0 + rows_of[scale : scale + 1]) + rows_of[shift : shift + 1]
    ).astype(BF16)


def weave(main, side, main_count, side_count):
    done = 0
    for index, _ in enumerate(main):
        due = -(-(index + 1) * side_count // main_count)
        while done < due:
            next(side, None)
            done += 1
    for _ in side:
        pass


def turn(source, target, tokens, width):
    for at in range(0, width, LANES):
        target[at : at + LANES, :] = source[:, at : at + LANES].T
        yield


def attention_pieces(turned_normed, input_turned, output_weight, same_position, places, groups, finish):
    query_rows, turned_keys, value_rows, kept, attended, turned_attended = places
    inner, width = output_weight.shape
    tokens = turned_normed.shape[1]
    head_size = inner // HEADS
    deep, tall = query_rows.shape[1], value_rows.shape[1]
    chunk = HEADS // 2
    scale = head_size ** (-0.5) * math.log2(math.e)

    def project(kind):
        rows = input_turned[kind * inner : (kind + 1) * inner]
        return jnp.dot(rows, turned_normed[...], preferred_element_type=F32)

    def keep_projected(kind, packed):
        for head in range(HEADS):
            values = packed[head * head_size : (head + 1) * head_size]
            if kind == 0:
                query_rows[head] = padded(normed_head(values, head_size, scale), 0.0, deep)
            elif kind == 1:
                turned_keys[head] = padded(normed_head(values, head_size, 1.0), 0.0, deep).T
            else:
                value_rows[head] = padded(values, 1.0, tall)

    pairs = [groups[at : at + 2] for at in range(0, len(groups), 2)]

    def over(pair):
        return slice(pair[0].start, pair[-1].stop)

    def score(head, pair):
        return jnp.dot(
            jnp.concatenate([turned_keys[head, group] for group in pair], 1),
            on_diagonal([query_rows[head, :, group] for group in pair]),
            preferred_element_type=F32,
        )

    def keep_scored(head, pair, scores):
        weights = jnp.exp2(scores).astype(BF16)
        if same_position is not None:
            weights = weights * same_position[:, : weights.shape[1]]
        kept[head, :, over(pair)] = weights

    def mix(head, pair):
        return jnp.dot(
            value_rows[head, :, over(pair)],
            on_diagonal([kept[head, :, group] for group in pair]),
            preferred_element_type=F32,
        )

    def keep_mixed(head, pair, mixed):
        rate = 1.0 / mixed[head_size : head_size + ROWS8]
        parts = mixed[:head_size].reshape(head_size // ROWS8, ROWS8, -1) * rate[None]
        first, last = head * head_size, (head + 1) * head_size
        columns = over(pair)
        attended[first:last, columns] = parts.reshape(head_size, -1)
        for at in range(0, inner, LANES):
            stop = min(at + LANES, inner)
            if first < stop <= last:
                turned_attended[columns, at:stop] = attended[at:stop, columns].astype(BF16).T

    def projections(kind):
        return (lambda: project(kind)), (lambda got: keep_projected(kind, got))

    def scorings(head, pair):
        return (lambda: score(head, pair)), (lambda got: keep_scored(head, pair, got))

    def mixings(head, pair):
        return (lambda: mix(head, pair)), (lambda got: keep_mixed(head, pair, got))

    def outputs(at):
        columns = slice(at, min(at + 2 * LANES, width))
        return (
            lambda: jnp.dot(
                turned_attended[...], output_weight[:, columns], preferred_element_type=F32
            )
        ), (lambda got: finish(columns, got))

    every = [(head, pair) for head in range(HEADS) for pair in pairs]
    scored = [scorings(*at) for at in every]
    mixes = [mixings(*at) for at in every]
    first = [projections(0), projections(1), projections(2), scored[0]]
    behind = scored[1:]
    for index, task in enumerate(behind):
        first.append(task)
        if index >= 1:
            first.append(mixes[index - 1])
    first += mixes[len(behind) - 1 :]
    for tasks in (first, [outputs(at) for at in range(0, width, 2 * LANES)]):
        waiting = None
        for issue, use in tasks:
            got = issue()
            if waiting is not None:
                waiting[0](waiting[1])
            waiting = (use, got)
            yield
        waiting[0](waiting[1])
        yield


def main_pieces(groups, width):
    return 3 + HEADS * -(-groups // 2) * 2 + 1 + -(-width // (2 * LANES)) + 1


def run_pipelined(steps, before, main, behind, main_count, before_count, behind_count):
    def one(index, own, last):
        following = jnp.minimum(index + 1, last)
        previous = jnp.maximum(index - 1, 0)
        side = itertools.chain(behind(previous, 1 - own), before(following, 1 - own))
        weave(main(index, own), side, main_count, before_count + behind_count)

    for _ in before(0, 0):
        pass
    if steps % 2 == 0:

        @pl.loop(0, steps // 2)
        def _(turn_index):
            one(2 * turn_index, 0, steps - 1)
            one(2 * turn_index + 1, 1, steps - 1)

        for _ in behind(steps - 1, 1):
            pass
    else:
        for index in range(steps):
            one(index, index % 2, steps - 1)
        for _ in behind(steps - 1, (steps - 1) % 2):
            pass


BLOCK = 32


def run_space(latent, embed, rows_of, input_weight, output_weight, out, places):
    frames, _, spatial = latent.shape
    width = embed.shape[1]
    step = groups_of(frames)
    tokens = step * spatial
    plain, turned, base, inner_places = places[0], places[1:3], places[3:5], places[5:]
    groups = [slice(at, at + spatial) for at in range(0, tokens, spatial)]

    def before(index, own):
        for frame in range(step):
            base[own][groups[frame]] = lax.dot_general(
                latent[index * step + frame].astype(BF16),
                embed[...],
                (((0,), (0,)), ((), ())),
                preferred_element_type=F32,
            )
            yield
        for at in range(0, tokens, BLOCK):
            plain[at : at + BLOCK] = modulated_norm(base[own][at : at + BLOCK], rows_of, 0, 1)
            yield
        yield from turn(plain, turned[own], tokens, width)

    def main(index, own):
        def finish(columns, mixed):
            after = base[own][:, columns] + rows_of[2:3, columns] * mixed
            for frame, group in enumerate(groups):
                out[index * step + frame, :, columns] = after[group].astype(out.dtype)

        return attention_pieces(
            turned[own], input_weight, output_weight, None, inner_places, groups, finish
        )

    def behind(index, own):
        return iter(())

    run_pipelined(
        frames // step, before, main, behind, main_pieces(step, width), step + tokens // BLOCK + width // LANES, 0
    )


def run_time(after, rows_of, input_weight, output_weight, final, out, places):
    frames, positions, width = after.shape
    step = groups_of(positions // ROWS8)
    rows = frames * ROWS8
    tokens = step * rows
    plain, turned, settled, inner_places = places[0], places[1:3], places[3:5], places[5:]
    groups = [slice(at, at + rows) for at in range(0, tokens, rows)]
    same_position = same_position_mask(frames, min(step, 2))

    def eight(index, group):
        at = (index * step + group) * ROWS8
        if not isinstance(at, int):
            at = pl.multiple_of(at, ROWS8)
        return pl.ds(at, ROWS8)

    def before(index, own):
        for group in range(step):
            for at in range(0, rows, BLOCK):
                some = slice(at // ROWS8, (at + BLOCK) // ROWS8)
                hidden = after[some, eight(index, group), :].reshape(BLOCK, width)
                first = groups[group].start + at
                plain[first : first + BLOCK] = modulated_norm(hidden, rows_of, 3, 4)
                yield
        yield from turn(plain, turned[own], tokens, width)

    def main(index, own):
        def finish(columns, mixed):
            for group in range(step):
                hidden = after[:, eight(index, group), columns].reshape(rows, -1)
                settled[own][groups[group], columns] = (
                    hidden + rows_of[5:6, columns] * mixed[groups[group]]
                )

        return attention_pieces(
            turned[own], input_weight, output_weight, same_position, inner_places, groups, finish
        )

    def behind(index, own):
        for group in range(step):
            for at in range(0, rows, BLOCK):
                first = groups[group].start + at
                normed = modulated_norm(settled[own][first : first + BLOCK], rows_of, 6, 7)
                predicted = lax.dot_general(
                    normed, final[...], (((1,), (1,)), ((), ())), preferred_element_type=F32
                )
                some = slice(at // ROWS8, (at + BLOCK) // ROWS8)
                out[some, eight(index, group), :] = predicted.reshape(
                    BLOCK // ROWS8, ROWS8, predicted.shape[1]
                )
                yield

    settled[1][...] = jnp.zeros_like(settled[1])
    run_pipelined(
        positions // (step * ROWS8), before, main, behind, main_pieces(step, width),
        tokens // BLOCK + width // LANES, tokens // BLOCK,
    )


def same_position_mask(frames, count):
    shape = (frames * ROWS8, count * frames * ROWS8)
    row = lax.broadcasted_iota(jnp.int32, shape, 0) % ROWS8
    column = lax.broadcasted_iota(jnp.int32, shape, 1) % ROWS8
    return jnp.where(row == column, 1.0, 0.0).astype(BF16)


def groups_of(blocks):
    return next(step for step in (4, 2, 1) if blocks % step == 0)


def fused_kernel(
    timestep, rate_state, rate_denoise, rate_noise, latent, noise, modulation, embed,
    space_in_hbm, space_out_hbm, time_in_hbm, time_out_hbm, final, increment, rounded,
    rows_of, space_in, space_out, time_in, time_out, after, staged, sems, *turned,
):
    own = timestep[0]
    copies = [
        pltpu.make_async_copy(source, target, sems.at[index])
        for index, (source, target) in enumerate(
            (
                (modulation.at[own], rows_of),
                (space_in_hbm, space_in),
                (space_out_hbm, space_out),
                (time_in_hbm, time_in),
                (time_out_hbm, time_out),
            )
        )
    ]
    for copy in copies:
        copy.start()
    for copy in copies[:3]:
        copy.wait()
    run_space(latent, embed, rows_of, space_in, space_out, after, turned)
    for copy in copies[3:]:
        copy.wait()
    run_time(after, rows_of, time_in, time_out, final, staged, turned)
    keep = rate_state[own] + jnp.where(own == 0, 1.0, 0.0)
    for frame in range(latent.shape[0]):
        value = (
            keep * latent[frame]
            + rate_denoise[own] * staged[frame].T
            + rate_noise[own] * noise[frame]
        )
        increment[frame] = value
        rounded[frame] = value.astype(BF16)


def space_kernel(latent, rows_of, embed, space_in, space_out, after, *turned):
    run_space(latent, embed, rows_of, space_in, space_out, after, turned)


def time_kernel(after, rows_of, time_in, time_out, final, predicted, *turned):
    run_time(after, rows_of, time_in, time_out, final, predicted, turned)


def vmem(count):
    return [pl.BlockSpec(memory_space=pltpu.VMEM)] * count


PARAMS = dict(compiler_params=pltpu.CompilerParams(vmem_limit_bytes=56 * 2**20))


def turned_scratch(tokens, group_rows, width, inner):
    head_size = inner // HEADS
    deep = -(-head_size // LANES) * LANES
    tall = head_size + ROWS16 - head_size % ROWS16
    return [
        pltpu.VMEM((tokens, width), BF16),
        pltpu.VMEM((width, tokens), BF16),
        pltpu.VMEM((width, tokens), BF16),
        pltpu.VMEM((tokens, width), F32),
        pltpu.VMEM((tokens, width), F32),
        pltpu.VMEM((HEADS, deep, tokens), BF16),
        pltpu.VMEM((HEADS, tokens, deep), BF16),
        pltpu.VMEM((HEADS, tall, tokens), BF16),
        pltpu.VMEM((HEADS, group_rows, tokens), BF16),
        pltpu.VMEM((inner, tokens), F32),
        pltpu.VMEM((tokens, inner), BF16),
    ]


def scalars(count):
    return [pl.BlockSpec(memory_space=pltpu.SMEM)] * count


def step_fused(timestep, rates, latent, noise, modulation, weights):
    frames, channels, spatial = latent.shape
    embed, space_in, space_out, time_in, time_out, final = weights
    width = embed.shape[1]
    return pl.pallas_call(
        fused_kernel,
        out_shape=[
            jax.ShapeDtypeStruct(latent.shape, F32),
            jax.ShapeDtypeStruct(latent.shape, BF16),
        ],
        in_specs=scalars(4)
        + vmem(2)
        + [pl.BlockSpec(memory_space=pl.ANY)]
        + vmem(1)
        + [pl.BlockSpec(memory_space=pl.ANY)] * 4
        + vmem(1),
        out_specs=vmem(2),
        scratch_shapes=[
            pltpu.VMEM(modulation.shape[1:], F32),
            pltpu.VMEM(space_in.shape, BF16),
            pltpu.VMEM(space_out.shape, BF16),
            pltpu.VMEM(time_in.shape, BF16),
            pltpu.VMEM(time_out.shape, BF16),
            pltpu.VMEM((frames, spatial, width), F32),
            pltpu.VMEM((frames, spatial, channels), F32),
            pltpu.SemaphoreType.DMA((5,)),
        ]
        + turned_scratch(groups_of(frames) * spatial, spatial, width, space_out.shape[0]),
        name="denoise",
        **PARAMS,
    )(
        timestep, *rates, latent, noise, modulation, embed, space_in, space_out, time_in,
        time_out, final,
    )


def step_split(timestep, rates, latent, noise, modulation, weights, peers):
    frames, channels, spatial = latent.shape
    embed, space_in, space_out, time_in, time_out, final = weights
    width = embed.shape[1]
    own = timestep[0]
    rows_of = lax.dynamic_index_in_dim(modulation, own, 0, keepdims=False)
    after = pl.pallas_call(
        space_kernel,
        out_shape=jax.ShapeDtypeStruct((frames, spatial, width), BF16),
        in_specs=vmem(5),
        out_specs=vmem(1)[0],
        scratch_shapes=turned_scratch(groups_of(frames) * spatial, spatial, width, space_out.shape[0]),
        name="space",
        **PARAMS,
    )(latent, rows_of, embed, space_in, space_out)
    after = lax.all_to_all(
        after, "tok", split_axis=1, concat_axis=0, tiled=True, axis_index_groups=peers
    )
    predicted = pl.pallas_call(
        time_kernel,
        out_shape=jax.ShapeDtypeStruct(after.shape[:2] + (channels,), F32),
        in_specs=vmem(5),
        out_specs=vmem(1)[0],
        scratch_shapes=turned_scratch(
            groups_of(after.shape[1] // ROWS8) * ROWS8 * after.shape[0], ROWS8 * after.shape[0],
            width, time_out.shape[0],
        ),
        name="time",
        **PARAMS,
    )(after.astype(F32), rows_of, time_in, time_out, final)
    predicted = lax.all_to_all(
        predicted, "tok", split_axis=0, concat_axis=1, tiled=True, axis_index_groups=peers
    )
    rate_state, rate_denoise, rate_noise = (rate[own] for rate in rates)
    increment = (
        (rate_state + jnp.where(own == 0, 1.0, 0.0)) * latent
        + rate_denoise * jnp.swapaxes(predicted, 1, 2)
        + rate_noise * noise
    )
    return increment, increment.astype(BF16)


RADIX = 4


def sum_before(values, held, timesteps, groups):
    before = jnp.zeros_like(values)
    reach = 1
    while reach < timesteps:
        arrived = []
        for back in range(reach, min(reach * RADIX, timesteps), reach):
            moves = [
                (step * groups + block, (step + back) * groups + block)
                for step in range(timesteps - back)
                for block in range(groups)
            ]
            arrived.append(lax.ppermute(held, "tok", moves))
        for part in arrived:
            before = before + part.astype(F32)
        held = (values + before).astype(BF16)
        reach *= RADIX
    return before


def body(
    initial_guess,
    noise_draws,
    drift_state,
    drift_denoise,
    noise_scale,
    modulation,
    embed_weight,
    space_input,
    space_output,
    time_input,
    time_output,
    final_weight,
):
    timesteps = modulation.shape[0]
    devices = lax.axis_size("tok")
    groups = devices // timesteps
    timestep = lax.axis_index("tok") // groups
    leading = timestep == 0
    own = timestep.astype(jnp.int32).reshape(1)
    if groups == 1:
        step = step_fused
    else:
        peers = [[row * groups + block for block in range(groups)] for row in range(timesteps)]
        step = functools.partial(step_split, peers=peers)
    rates = (drift_state, drift_denoise, noise_scale)
    weights = (
        embed_weight, space_input.T, space_output, time_input.T, time_output, final_weight.T
    )
    latent = initial_guess
    result = initial_guess
    for _ in range(ITERS):
        increment, rounded = step(own, rates, latent, noise_draws, modulation, weights)
        before = sum_before(increment, rounded, timesteps, groups)
        result = before + increment
        latent = jnp.where(leading, latent, before)
    return result


def solution(mesh):
    rows = P(("group", "tok"), None, None)
    placed = (rows, rows) + (P(),) * 10
    return jax.shard_map(
        body, mesh=mesh, in_specs=placed, out_specs=rows, check_vma=False
    )
```

```python
import functools
import itertools
import math

import jax
import jax.numpy as jnp
from jax import lax
from jax.experimental import pallas as pl
from jax.experimental.pallas import tpu as pltpu
from jax.sharding import PartitionSpec as P

HEADS = 8
ITERS = 2
LANES = 128
ROWS8 = 8
ROWS16 = 16
F32 = jnp.float32
BF16 = jnp.bfloat16


def layer_norm(values):
    center = values - jnp.mean(values, -1, keepdims=True)
    return center * lax.rsqrt(jnp.mean(center * center, -1, keepdims=True) + 1e-06)


def normed_head(values, head_size, scale):
    total = jnp.sum(values * values, 0, keepdims=True)
    return values * (lax.rsqrt(total * (1.0 / head_size) + 1e-06) * scale)


def padded(values, fill, rows):
    extra = rows - values.shape[0]
    return jnp.concatenate(
        [values, jnp.full((extra, values.shape[1]), fill, F32)], 0
    ).astype(BF16)


def on_diagonal(blocks):
    zero = jnp.zeros_like(blocks[0])
    return jnp.concatenate(
        [
            jnp.concatenate([block if at == own else zero for at in range(len(blocks))], 1)
            for own, block in enumerate(blocks)
        ],
        0,
    )


def modulated_norm(values, rows_of, shift, scale):
    return (
        layer_norm(values) * (1.0 + rows_of[scale : scale + 1]) + rows_of[shift : shift + 1]
    ).astype(BF16)


def weave(main, side, main_count, side_count):
    done = 0
    for index, _ in enumerate(main):
        due = -(-(index + 1) * side_count // main_count)
        while done < due:
            next(side, None)
            done += 1
    for _ in side:
        pass


def attention_pieces(normed, input_turned, output_weight, same_position, places, groups, finish):
    query_rows, turned_keys, value_rows, kept, attended, turned_attended = places
    inner, width = output_weight.shape
    tokens = normed.shape[0]
    head_size = inner // HEADS
    deep, tall = query_rows.shape[1], value_rows.shape[1]
    chunk = HEADS // 2
    scale = head_size ** (-0.5) * math.log2(math.e)

    def project(kind):
        rows = input_turned[kind * inner : (kind + 1) * inner]
        return lax.dot_general(
            rows, normed[...], (((1,), (1,)), ((), ())), preferred_element_type=F32
        )

    def keep_projected(kind, packed):
        for head in range(HEADS):
            values = packed[head * head_size : (head + 1) * head_size]
            if kind == 0:
                query_rows[head] = padded(normed_head(values, head_size, scale), 0.0, deep)
            elif kind == 1:
                turned_keys[head] = padded(normed_head(values, head_size, 1.0), 0.0, deep).T
            else:
                value_rows[head] = padded(values, 1.0, tall)

    pairs = [groups[at : at + 2] for at in range(0, len(groups), 2)]

    def over(pair):
        return slice(pair[0].start, pair[-1].stop)

    def score(head, pair):
        return jnp.dot(
            jnp.concatenate([turned_keys[head, group] for group in pair], 1),
            on_diagonal([query_rows[head, :, group] for group in pair]),
            preferred_element_type=F32,
        )

    def keep_scored(head, pair, scores):
        weights = jnp.exp2(scores).astype(BF16)
        if same_position is not None:
            weights = weights * same_position[:, : weights.shape[1]]
        kept[head, :, over(pair)] = weights

    def mix(head, pair):
        return jnp.dot(
            value_rows[head, :, over(pair)],
            on_diagonal([kept[head, :, group] for group in pair]),
            preferred_element_type=F32,
        )

    def keep_mixed(head, pair, mixed):
        rate = 1.0 / mixed[head_size : head_size + ROWS8]
        parts = mixed[:head_size].reshape(head_size // ROWS8, ROWS8, -1) * rate[None]
        first, last = head * head_size, (head + 1) * head_size
        columns = over(pair)
        attended[first:last, columns] = parts.reshape(head_size, -1)
        for at in range(0, inner, LANES):
            stop = min(at + LANES, inner)
            if first < stop <= last:
                turned_attended[columns, at:stop] = attended[at:stop, columns].astype(BF16).T

    def projections(kind):
        return (lambda: project(kind)), (lambda got: keep_projected(kind, got))

    def scorings(head, pair):
        return (lambda: score(head, pair)), (lambda got: keep_scored(head, pair, got))

    def mixings(head, pair):
        return (lambda: mix(head, pair)), (lambda got: keep_mixed(head, pair, got))

    def outputs(at):
        columns = slice(at, min(at + 2 * LANES, width))
        return (
            lambda: jnp.dot(
                turned_attended[...], output_weight[:, columns], preferred_element_type=F32
            )
        ), (lambda got: finish(columns, got))

    every = [(head, pair) for head in range(HEADS) for pair in pairs]
    scored = [scorings(*at) for at in every]
    mixes = [mixings(*at) for at in every]
    first = [projections(0), projections(1), projections(2), scored[0]]
    behind = scored[1:]
    for index, task in enumerate(behind):
        first.append(task)
        if index >= 1:
            first.append(mixes[index - 1])
    first += mixes[len(behind) - 1 :]
    for tasks in (first, [outputs(at) for at in range(0, width, 2 * LANES)]):
        waiting = None
        for issue, use in tasks:
            got = issue()
            if waiting is not None:
                waiting[0](waiting[1])
            waiting = (use, got)
            yield
        waiting[0](waiting[1])
        yield


def main_pieces(groups, width):
    return 3 + HEADS * -(-groups // 2) * 2 + 1 + -(-width // (2 * LANES)) + 1


def run_pipelined(steps, before, main, behind, main_count, before_count, behind_count, ready):
    def one(index, own, last):
        following = jnp.minimum(index + 1, last)
        previous = jnp.maximum(index - 1, 0)
        side = itertools.chain(behind(previous, 1 - own), before(following, 1 - own))
        weave(main(index, own), side, main_count, before_count + behind_count)

    for _ in before(0, 0):
        pass
    ready()
    if steps % 2 == 0:

        @pl.loop(0, steps // 2)
        def _(turn_index):
            one(2 * turn_index, 0, steps - 1)
            one(2 * turn_index + 1, 1, steps - 1)

        for _ in behind(steps - 1, 1):
            pass
    else:
        for index in range(steps):
            one(index, index % 2, steps - 1)
        for _ in behind(steps - 1, (steps - 1) % 2):
            pass


BLOCK = 32


def run_space(latent, embed, rows_of, input_weight, output_weight, out, places, ready):
    frames, _, spatial = latent.shape
    width = embed.shape[1]
    step = groups_of(frames)
    tokens = step * spatial
    normed, base, inner_places = places[:2], places[2:4], places[4:]
    groups = [slice(at, at + spatial) for at in range(0, tokens, spatial)]

    def before(index, own):
        for frame in range(step):
            base[own][groups[frame]] = lax.dot_general(
                latent[index * step + frame].astype(BF16),
                embed[...],
                (((0,), (0,)), ((), ())),
                preferred_element_type=F32,
            )
            yield
        for at in range(0, tokens, BLOCK):
            normed[own][at : at + BLOCK] = modulated_norm(
                base[own][at : at + BLOCK], rows_of, 0, 1
            )
            yield

    def main(index, own):
        def finish(columns, mixed):
            after = base[own][:, columns] + rows_of[2:3, columns] * mixed
            for frame, group in enumerate(groups):
                out[index * step + frame, :, columns] = after[group].astype(out.dtype)

        return attention_pieces(
            normed[own], input_weight, output_weight, None, inner_places, groups, finish
        )

    def behind(index, own):
        return iter(())

    run_pipelined(
        frames // step, before, main, behind, main_pieces(step, width), step + tokens // BLOCK, 0, ready
    )


def run_time(after, rows_of, input_weight, output_weight, final, out, places, ready):
    frames, positions, width = after.shape
    step = groups_of(positions // ROWS8)
    rows = frames * ROWS8
    tokens = step * rows
    normed, settled, inner_places = places[:2], places[2:4], places[4:]
    groups = [slice(at, at + rows) for at in range(0, tokens, rows)]
    same_position = same_position_mask(frames, min(step, 2))

    def eight(index, group):
        at = (index * step + group) * ROWS8
        if not isinstance(at, int):
            at = pl.multiple_of(at, ROWS8)
        return pl.ds(at, ROWS8)

    def before(index, own):
        for group in range(step):
            for at in range(0, rows, BLOCK):
                some = slice(at // ROWS8, (at + BLOCK) // ROWS8)
                hidden = after[some, eight(index, group), :].reshape(BLOCK, width)
                first = groups[group].start + at
                normed[own][first : first + BLOCK] = modulated_norm(hidden, rows_of, 3, 4)
                yield

    def main(index, own):
        def finish(columns, mixed):
            for group in range(step):
                hidden = after[:, eight(index, group), columns].reshape(rows, -1)
                settled[own][groups[group], columns] = (
                    hidden + rows_of[5:6, columns] * mixed[groups[group]]
                )

        return attention_pieces(
            normed[own], input_weight, output_weight, same_position, inner_places, groups, finish
        )

    def behind(index, own):
        for group in range(step):
            for at in range(0, rows, BLOCK):
                first = groups[group].start + at
                last = modulated_norm(settled[own][first : first + BLOCK], rows_of, 6, 7)
                predicted = lax.dot_general(
                    last, final[...], (((1,), (1,)), ((), ())), preferred_element_type=F32
                )
                some = slice(at // ROWS8, (at + BLOCK) // ROWS8)
                out[some, eight(index, group), :] = predicted.reshape(
                    BLOCK // ROWS8, ROWS8, predicted.shape[1]
                )
                yield

    settled[1][...] = jnp.zeros_like(settled[1])
    run_pipelined(
        positions // (step * ROWS8), before, main, behind, main_pieces(step, width),
        tokens // BLOCK, tokens // BLOCK, ready,
    )


def same_position_mask(frames, count):
    shape = (frames * ROWS8, count * frames * ROWS8)
    row = lax.broadcasted_iota(jnp.int32, shape, 0) % ROWS8
    column = lax.broadcasted_iota(jnp.int32, shape, 1) % ROWS8
    return jnp.where(row == column, 1.0, 0.0).astype(BF16)


def groups_of(blocks):
    return next(step for step in (4, 2, 1) if blocks % step == 0)


def fused_kernel(
    timestep, rate_state, rate_denoise, rate_noise, latent, noise, modulation, embed,
    space_in_hbm, space_out_hbm, time_in_hbm, time_out_hbm, final, increment, rounded,
    rows_of, space_in, space_out, time_in, time_out, after, staged, sems, *turned,
):
    own = timestep[0]
    copies = [
        pltpu.make_async_copy(source, target, sems.at[index])
        for index, (source, target) in enumerate(
            (
                (modulation.at[own], rows_of),
                (space_in_hbm, space_in),
                (space_out_hbm, space_out),
                (time_in_hbm, time_in),
                (time_out_hbm, time_out),
            )
        )
    ]
    for copy in copies:
        copy.start()

    def wait_for(some):
        for copy in some:
            copy.wait()

    wait_for(copies[:1])
    run_space(
        latent, embed, rows_of, space_in, space_out, after, turned, lambda: wait_for(copies[1:3])
    )
    run_time(
        after, rows_of, time_in, time_out, final, staged, turned, lambda: wait_for(copies[3:])
    )
    keep = rate_state[own] + jnp.where(own == 0, 1.0, 0.0)
    for frame in range(latent.shape[0]):
        value = (
            keep * latent[frame]
            + rate_denoise[own] * staged[frame].T
            + rate_noise[own] * noise[frame]
        )
        increment[frame] = value
        rounded[frame] = value.astype(BF16)


def space_kernel(latent, rows_of, embed, space_in, space_out, after, *turned):
    run_space(latent, embed, rows_of, space_in, space_out, after, turned, lambda: None)


def time_kernel(after, rows_of, time_in, time_out, final, predicted, *turned):
    run_time(after, rows_of, time_in, time_out, final, predicted, turned, lambda: None)


def vmem(count):
    return [pl.BlockSpec(memory_space=pltpu.VMEM)] * count


PARAMS = dict(compiler_params=pltpu.CompilerParams(vmem_limit_bytes=56 * 2**20))


def turned_scratch(tokens, group_rows, width, inner):
    head_size = inner // HEADS
    deep = -(-head_size // LANES) * LANES
    tall = head_size + ROWS16 - head_size % ROWS16
    return [
        pltpu.VMEM((tokens, width), BF16),
        pltpu.VMEM((tokens, width), BF16),
        pltpu.VMEM((tokens, width), F32),
        pltpu.VMEM((tokens, width), F32),
        pltpu.VMEM((HEADS, deep, tokens), BF16),
        pltpu.VMEM((HEADS, tokens, deep), BF16),
        pltpu.VMEM((HEADS, tall, tokens), BF16),
        pltpu.VMEM((HEADS, group_rows, tokens), BF16),
        pltpu.VMEM((inner, tokens), F32),
        pltpu.VMEM((tokens, inner), BF16),
    ]


def scalars(count):
    return [pl.BlockSpec(memory_space=pltpu.SMEM)] * count


def step_fused(timestep, rates, latent, noise, modulation, weights):
    frames, channels, spatial = latent.shape
    embed, space_in, space_out, time_in, time_out, final = weights
    width = embed.shape[1]
    return pl.pallas_call(
        fused_kernel,
        out_shape=[
            jax.ShapeDtypeStruct(latent.shape, F32),
            jax.ShapeDtypeStruct(latent.shape, BF16),
        ],
        in_specs=scalars(4)
        + vmem(2)
        + [pl.BlockSpec(memory_space=pl.ANY)]
        + vmem(1)
        + [pl.BlockSpec(memory_space=pl.ANY)] * 4
        + vmem(1),
        out_specs=vmem(2),
        scratch_shapes=[
            pltpu.VMEM(modulation.shape[1:], F32),
            pltpu.VMEM(space_in.shape, BF16),
            pltpu.VMEM(space_out.shape, BF16),
            pltpu.VMEM(time_in.shape, BF16),
            pltpu.VMEM(time_out.shape, BF16),
            pltpu.VMEM((frames, spatial, width), F32),
            pltpu.VMEM((frames, spatial, channels), F32),
            pltpu.SemaphoreType.DMA((5,)),
        ]
        + turned_scratch(groups_of(frames) * spatial, spatial, width, space_out.shape[0]),
        name="denoise",
        **PARAMS,
    )(
        timestep, *rates, latent, noise, modulation, embed, space_in, space_out, time_in,
        time_out, final,
    )


def step_split(timestep, rates, latent, noise, modulation, weights, peers):
    frames, channels, spatial = latent.shape
    embed, space_in, space_out, time_in, time_out, final = weights
    width = embed.shape[1]
    own = timestep[0]
    rows_of = lax.dynamic_index_in_dim(modulation, own, 0, keepdims=False)
    after = pl.pallas_call(
        space_kernel,
        out_shape=jax.ShapeDtypeStruct((frames, spatial, width), BF16),
        in_specs=vmem(5),
        out_specs=vmem(1)[0],
        scratch_shapes=turned_scratch(groups_of(frames) * spatial, spatial, width, space_out.shape[0]),
        name="space",
        **PARAMS,
    )(latent, rows_of, embed, space_in, space_out)
    after = lax.all_to_all(
        after, "tok", split_axis=1, concat_axis=0, tiled=True, axis_index_groups=peers
    )
    predicted = pl.pallas_call(
        time_kernel,
        out_shape=jax.ShapeDtypeStruct(after.shape[:2] + (channels,), F32),
        in_specs=vmem(5),
        out_specs=vmem(1)[0],
        scratch_shapes=turned_scratch(
            groups_of(after.shape[1] // ROWS8) * ROWS8 * after.shape[0], ROWS8 * after.shape[0],
            width, time_out.shape[0],
        ),
        name="time",
        **PARAMS,
    )(after.astype(F32), rows_of, time_in, time_out, final)
    predicted = lax.all_to_all(
        predicted, "tok", split_axis=0, concat_axis=1, tiled=True, axis_index_groups=peers
    )
    rate_state, rate_denoise, rate_noise = (rate[own] for rate in rates)
    increment = (
        (rate_state + jnp.where(own == 0, 1.0, 0.0)) * latent
        + rate_denoise * jnp.swapaxes(predicted, 1, 2)
        + rate_noise * noise
    )
    return increment, increment.astype(BF16)


RADIX = 4


def sum_before(values, held, timesteps, groups):
    before = jnp.zeros_like(values)
    reach = 1
    while reach < timesteps:
        arrived = []
        for back in range(reach, min(reach * RADIX, timesteps), reach):
            moves = [
                (step * groups + block, (step + back) * groups + block)
                for step in range(timesteps - back)
                for block in range(groups)
            ]
            arrived.append(lax.ppermute(held, "tok", moves))
        for part in arrived:
            before = before + part.astype(F32)
        held = (values + before).astype(BF16)
        reach *= RADIX
    return before


def body(
    initial_guess,
    noise_draws,
    drift_state,
    drift_denoise,
    noise_scale,
    modulation,
    embed_weight,
    space_input,
    space_output,
    time_input,
    time_output,
    final_weight,
):
    timesteps = modulation.shape[0]
    devices = lax.axis_size("tok")
    groups = devices // timesteps
    timestep = lax.axis_index("tok") // groups
    leading = timestep == 0
    own = timestep.astype(jnp.int32).reshape(1)
    if groups == 1:
        step = step_fused
    else:
        peers = [[row * groups + block for block in range(groups)] for row in range(timesteps)]
        step = functools.partial(step_split, peers=peers)
    rates = (drift_state, drift_denoise, noise_scale)
    weights = (
        embed_weight, space_input.T, space_output, time_input.T, time_output, final_weight.T
    )

    def iterate(_, held):
        latent = held[0]
        increment, rounded = step(own, rates, latent, noise_draws, modulation, weights)
        before = sum_before(increment, rounded, timesteps, groups)
        return jnp.where(leading, latent, before), before + increment

    return lax.fori_loop(0, ITERS, iterate, (initial_guess, initial_guess))[1]


def solution(mesh):
    rows = P(("group", "tok"), None, None)
    placed = (rows, rows) + (P(),) * 10
    return jax.shard_map(
        body, mesh=mesh, in_specs=placed, out_specs=rows, check_vma=False
    )
```

```python
import functools
import itertools
import math

import jax
import jax.numpy as jnp
from jax import lax
from jax.experimental import pallas as pl
from jax.experimental.pallas import tpu as pltpu
from jax.sharding import PartitionSpec as P

HEADS = 8
ITERS = 2
LANES = 128
ROWS8 = 8
ROWS16 = 16
F32 = jnp.float32
BF16 = jnp.bfloat16


def layer_norm(values):
    center = values - jnp.mean(values, -1, keepdims=True)
    return center * lax.rsqrt(jnp.mean(center * center, -1, keepdims=True) + 1e-06)


def normed_head(values, head_size, scale):
    total = jnp.sum(values * values, 0, keepdims=True)
    return values * (lax.rsqrt(total * (1.0 / head_size) + 1e-06) * scale)


def padded(values, fill, rows):
    extra = rows - values.shape[0]
    return jnp.concatenate(
        [values, jnp.full((extra, values.shape[1]), fill, F32)], 0
    ).astype(BF16)


def on_diagonal(blocks):
    zero = jnp.zeros_like(blocks[0])
    return jnp.concatenate(
        [
            jnp.concatenate([block if at == own else zero for at in range(len(blocks))], 1)
            for own, block in enumerate(blocks)
        ],
        0,
    )


def modulated_norm(values, rows_of, shift, scale):
    return (
        layer_norm(values) * (1.0 + rows_of[scale : scale + 1]) + rows_of[shift : shift + 1]
    ).astype(BF16)


def weave(main, side, main_count, side_count):
    done = 0
    for index, _ in enumerate(main):
        due = -(-(index + 1) * side_count // main_count)
        while done < due:
            next(side, None)
            done += 1
    for _ in side:
        pass


def attention_pieces(normed, input_turned, output_weight, same_position, places, groups, finish):
    query_rows, turned_keys, value_rows, kept, attended, turned_attended = places
    inner, width = output_weight.shape
    tokens = normed.shape[0]
    head_size = inner // HEADS
    deep, tall = query_rows.shape[1], value_rows.shape[1]
    chunk = HEADS // 2
    scale = head_size ** (-0.5) * math.log2(math.e)

    def project(kind):
        rows = input_turned[kind * inner : (kind + 1) * inner]
        return lax.dot_general(
            rows, normed[...], (((1,), (1,)), ((), ())), preferred_element_type=F32
        )

    def keep_projected(kind, packed):
        for head in range(HEADS):
            values = packed[head * head_size : (head + 1) * head_size]
            if kind == 0:
                query_rows[head] = padded(normed_head(values, head_size, scale), 0.0, deep)
            elif kind == 1:
                turned_keys[head] = padded(normed_head(values, head_size, 1.0), 0.0, deep).T
            else:
                value_rows[head] = padded(values, 1.0, tall)

    pairs = [groups[at : at + 2] for at in range(0, len(groups), 2)]

    def over(pair):
        return slice(pair[0].start, pair[-1].stop)

    def score(head, pair):
        return jnp.dot(
            jnp.concatenate([turned_keys[head, group] for group in pair], 1),
            on_diagonal([query_rows[head, :, group] for group in pair]),
            preferred_element_type=F32,
        )

    def keep_scored(head, pair, scores):
        weights = jnp.exp2(scores).astype(BF16)
        if same_position is not None:
            weights = weights * same_position[:, : weights.shape[1]]
        kept[head, :, over(pair)] = weights

    def mix(head, pair):
        return jnp.dot(
            value_rows[head, :, over(pair)],
            on_diagonal([kept[head, :, group] for group in pair]),
            preferred_element_type=F32,
        )

    def keep_mixed(head, pair, mixed):
        rate = 1.0 / mixed[head_size : head_size + ROWS8]
        parts = mixed[:head_size].reshape(head_size // ROWS8, ROWS8, -1) * rate[None]
        first, last = head * head_size, (head + 1) * head_size
        columns = over(pair)
        attended[first:last, columns] = parts.reshape(head_size, -1)
        for at in range(0, inner, LANES):
            stop = min(at + LANES, inner)
            if first < stop <= last:
                turned_attended[columns, at:stop] = attended[at:stop, columns].astype(BF16).T

    def projections(kind):
        return (lambda: project(kind)), (lambda got: keep_projected(kind, got))

    def scorings(head, pair):
        return (lambda: score(head, pair)), (lambda got: keep_scored(head, pair, got))

    def mixings(head, pair):
        return (lambda: mix(head, pair)), (lambda got: keep_mixed(head, pair, got))

    def outputs(at):
        columns = slice(at, min(at + 2 * LANES, width))
        return (
            lambda: jnp.dot(
                turned_attended[...], output_weight[:, columns], preferred_element_type=F32
            )
        ), (lambda got: finish(columns, got))

    every = [(head, pair) for head in range(HEADS) for pair in pairs]
    scored = [scorings(*at) for at in every]
    mixes = [mixings(*at) for at in every]
    first = [projections(0), projections(1), projections(2), scored[0]]
    behind = scored[1:]
    for index, task in enumerate(behind):
        first.append(task)
        if index >= 1:
            first.append(mixes[index - 1])
    first += mixes[len(behind) - 1 :]
    for tasks in (first, [outputs(at) for at in range(0, width, 2 * LANES)]):
        waiting = None
        for issue, use in tasks:
            got = issue()
            if waiting is not None:
                waiting[0](waiting[1])
            waiting = (use, got)
            yield
        waiting[0](waiting[1])
        yield


def main_pieces(groups, width):
    return 3 + HEADS * -(-groups // 2) * 2 + 1 + -(-width // (2 * LANES)) + 1


def run_pipelined(steps, before, main, behind, main_count, before_count, behind_count, ready):
    def one(index, own, last):
        following = jnp.minimum(index + 1, last)
        previous = jnp.maximum(index - 1, 0)
        side = itertools.chain(behind(previous, 1 - own), before(following, 1 - own))
        weave(main(index, own), side, main_count, before_count + behind_count)

    for _ in before(0, 0):
        pass
    ready()
    if steps % 2 == 0:

        @pl.loop(0, steps // 2)
        def _(turn_index):
            one(2 * turn_index, 0, steps - 1)
            one(2 * turn_index + 1, 1, steps - 1)

        for _ in behind(steps - 1, 1):
            pass
    else:
        for index in range(steps):
            one(index, index % 2, steps - 1)
        for _ in behind(steps - 1, (steps - 1) % 2):
            pass


BLOCK = 32


def run_space(latent, embed, rows_of, input_weight, output_weight, out, places, ready):
    frames, _, spatial = latent.shape
    width = embed.shape[1]
    step = groups_of(frames)
    tokens = step * spatial
    normed, base, inner_places = places[:2], places[2:4], places[5:]
    groups = [slice(at, at + spatial) for at in range(0, tokens, spatial)]

    def before(index, own):
        for frame in range(step):
            base[own][groups[frame]] = lax.dot_general(
                latent[index * step + frame].astype(BF16),
                embed[...],
                (((0,), (0,)), ((), ())),
                preferred_element_type=F32,
            )
            yield
        for at in range(0, tokens, BLOCK):
            normed[own][at : at + BLOCK] = modulated_norm(
                base[own][at : at + BLOCK], rows_of, 0, 1
            )
            yield

    def main(index, own):
        def finish(columns, mixed):
            after = base[own][:, columns] + rows_of[2:3, columns] * mixed
            for frame, group in enumerate(groups):
                out[index * step + frame, :, columns] = after[group].astype(out.dtype)

        return attention_pieces(
            normed[own], input_weight, output_weight, None, inner_places, groups, finish
        )

    def behind(index, own):
        return iter(())

    run_pipelined(
        frames // step, before, main, behind, main_pieces(step, width), step + tokens // BLOCK, 0, ready
    )


def run_time(after, rows_of, input_weight, output_weight, final, out, places, ready):
    frames, positions, width = after.shape
    step = groups_of(positions // ROWS8)
    rows = frames * ROWS8
    tokens = step * rows
    normed, settled, last, inner_places = places[:2], places[2:4], places[4], places[5:]
    groups = [slice(at, at + rows) for at in range(0, tokens, rows)]
    same_position = same_position_mask(frames, min(step, 2))

    def eight(index, group):
        at = (index * step + group) * ROWS8
        if not isinstance(at, int):
            at = pl.multiple_of(at, ROWS8)
        return pl.ds(at, ROWS8)

    def before(index, own):
        for group in range(step):
            for at in range(0, rows, BLOCK):
                some = slice(at // ROWS8, (at + BLOCK) // ROWS8)
                hidden = after[some, eight(index, group), :].reshape(BLOCK, width)
                first = groups[group].start + at
                normed[own][first : first + BLOCK] = modulated_norm(hidden, rows_of, 3, 4)
                yield

    def main(index, own):
        def finish(columns, mixed):
            for group in range(step):
                hidden = after[:, eight(index, group), columns].reshape(rows, -1)
                settled[own][groups[group], columns] = (
                    hidden + rows_of[5:6, columns] * mixed[groups[group]]
                )

        return attention_pieces(
            normed[own], input_weight, output_weight, same_position, inner_places, groups, finish
        )

    def behind(index, own):
        for at in range(0, tokens, BLOCK):
            last[at : at + BLOCK] = modulated_norm(settled[own][at : at + BLOCK], rows_of, 6, 7)
            yield
        predicted = lax.dot_general(
            final[...], last[...], (((1,), (1,)), ((), ())), preferred_element_type=F32
        )
        for group in range(step):
            part = predicted[:, groups[group]].T
            out[:, eight(index, group), :] = part.reshape(frames, ROWS8, part.shape[1])
        yield

    settled[1][...] = jnp.zeros_like(settled[1])
    run_pipelined(
        positions // (step * ROWS8), before, main, behind, main_pieces(step, width),
        tokens // BLOCK, tokens // BLOCK + 1, ready,
    )


def same_position_mask(frames, count):
    shape = (frames * ROWS8, count * frames * ROWS8)
    row = lax.broadcasted_iota(jnp.int32, shape, 0) % ROWS8
    column = lax.broadcasted_iota(jnp.int32, shape, 1) % ROWS8
    return jnp.where(row == column, 1.0, 0.0).astype(BF16)


def groups_of(blocks):
    return next(step for step in (4, 2, 1) if blocks % step == 0)


def fused_kernel(
    timestep, rate_state, rate_denoise, rate_noise, latent, noise, modulation, embed,
    space_in_hbm, space_out_hbm, time_in_hbm, time_out_hbm, final, increment, rounded,
    rows_of, space_in, space_out, time_in, time_out, after, staged, sems, *turned,
):
    own = timestep[0]
    copies = [
        pltpu.make_async_copy(source, target, sems.at[index])
        for index, (source, target) in enumerate(
            (
                (modulation.at[own], rows_of),
                (space_in_hbm, space_in),
                (space_out_hbm, space_out),
                (time_in_hbm, time_in),
                (time_out_hbm, time_out),
            )
        )
    ]
    for copy in copies:
        copy.start()

    def wait_for(some):
        for copy in some:
            copy.wait()

    wait_for(copies[:1])
    run_space(
        latent, embed, rows_of, space_in, space_out, after, turned, lambda: wait_for(copies[1:3])
    )
    run_time(
        after, rows_of, time_in, time_out, final, staged, turned, lambda: wait_for(copies[3:])
    )
    keep = rate_state[own] + jnp.where(own == 0, 1.0, 0.0)
    for frame in range(latent.shape[0]):
        value = (
            keep * latent[frame]
            + rate_denoise[own] * staged[frame].T
            + rate_noise[own] * noise[frame]
        )
        increment[frame] = value
        rounded[frame] = value.astype(BF16)


def space_kernel(latent, rows_of, embed, space_in, space_out, after, *turned):
    run_space(latent, embed, rows_of, space_in, space_out, after, turned, lambda: None)


def time_kernel(after, rows_of, time_in, time_out, final, predicted, *turned):
    run_time(after, rows_of, time_in, time_out, final, predicted, turned, lambda: None)


def vmem(count):
    return [pl.BlockSpec(memory_space=pltpu.VMEM)] * count


PARAMS = dict(compiler_params=pltpu.CompilerParams(vmem_limit_bytes=56 * 2**20))


def turned_scratch(tokens, group_rows, width, inner):
    head_size = inner // HEADS
    deep = -(-head_size // LANES) * LANES
    tall = head_size + ROWS16 - head_size % ROWS16
    return [
        pltpu.VMEM((tokens, width), BF16),
        pltpu.VMEM((tokens, width), BF16),
        pltpu.VMEM((tokens, width), F32),
        pltpu.VMEM((tokens, width), F32),
        pltpu.VMEM((tokens, width), BF16),
        pltpu.VMEM((HEADS, deep, tokens), BF16),
        pltpu.VMEM((HEADS, tokens, deep), BF16),
        pltpu.VMEM((HEADS, tall, tokens), BF16),
        pltpu.VMEM((HEADS, group_rows, tokens), BF16),
        pltpu.VMEM((inner, tokens), F32),
        pltpu.VMEM((tokens, inner), BF16),
    ]


def scalars(count):
    return [pl.BlockSpec(memory_space=pltpu.SMEM)] * count


def step_fused(timestep, rates, latent, noise, modulation, weights):
    frames, channels, spatial = latent.shape
    embed, space_in, space_out, time_in, time_out, final = weights
    width = embed.shape[1]
    return pl.pallas_call(
        fused_kernel,
        out_shape=[
            jax.ShapeDtypeStruct(latent.shape, F32),
            jax.ShapeDtypeStruct(latent.shape, BF16),
        ],
        in_specs=scalars(4)
        + vmem(2)
        + [pl.BlockSpec(memory_space=pl.ANY)]
        + vmem(1)
        + [pl.BlockSpec(memory_space=pl.ANY)] * 4
        + vmem(1),
        out_specs=vmem(2),
        scratch_shapes=[
            pltpu.VMEM(modulation.shape[1:], F32),
            pltpu.VMEM(space_in.shape, BF16),
            pltpu.VMEM(space_out.shape, BF16),
            pltpu.VMEM(time_in.shape, BF16),
            pltpu.VMEM(time_out.shape, BF16),
            pltpu.VMEM((frames, spatial, width), F32),
            pltpu.VMEM((frames, spatial, channels), F32),
            pltpu.SemaphoreType.DMA((5,)),
        ]
        + turned_scratch(groups_of(frames) * spatial, spatial, width, space_out.shape[0]),
        name="denoise",
        **PARAMS,
    )(
        timestep, *rates, latent, noise, modulation, embed, space_in, space_out, time_in,
        time_out, final,
    )


def step_split(timestep, rates, latent, noise, modulation, weights, peers):
    frames, channels, spatial = latent.shape
    embed, space_in, space_out, time_in, time_out, final = weights
    width = embed.shape[1]
    own = timestep[0]
    rows_of = lax.dynamic_index_in_dim(modulation, own, 0, keepdims=False)
    after = pl.pallas_call(
        space_kernel,
        out_shape=jax.ShapeDtypeStruct((frames, spatial, width), BF16),
        in_specs=vmem(5),
        out_specs=vmem(1)[0],
        scratch_shapes=turned_scratch(groups_of(frames) * spatial, spatial, width, space_out.shape[0]),
        name="space",
        **PARAMS,
    )(latent, rows_of, embed, space_in, space_out)
    after = lax.all_to_all(
        after, "tok", split_axis=1, concat_axis=0, tiled=True, axis_index_groups=peers
    )
    predicted = pl.pallas_call(
        time_kernel,
        out_shape=jax.ShapeDtypeStruct(after.shape[:2] + (channels,), F32),
        in_specs=vmem(5),
        out_specs=vmem(1)[0],
        scratch_shapes=turned_scratch(
            groups_of(after.shape[1] // ROWS8) * ROWS8 * after.shape[0], ROWS8 * after.shape[0],
            width, time_out.shape[0],
        ),
        name="time",
        **PARAMS,
    )(after.astype(F32), rows_of, time_in, time_out, final)
    predicted = lax.all_to_all(
        predicted, "tok", split_axis=0, concat_axis=1, tiled=True, axis_index_groups=peers
    )
    rate_state, rate_denoise, rate_noise = (rate[own] for rate in rates)
    increment = (
        (rate_state + jnp.where(own == 0, 1.0, 0.0)) * latent
        + rate_denoise * jnp.swapaxes(predicted, 1, 2)
        + rate_noise * noise
    )
    return increment, increment.astype(BF16)


def earlier_kernel(parts, sums):
    total = jnp.zeros(parts.shape[1:], F32)
    for step in range(parts.shape[0]):
        sums[step] = total.astype(BF16)
        total = total + parts[step].astype(F32)


def sum_before(held, timesteps, groups):
    frames, channels, spatial = held.shape
    rows = frames * channels
    peers = None
    if groups > 1:
        peers = [[step * groups + block for step in range(timesteps)] for block in range(groups)]
    swap = functools.partial(
        lax.all_to_all, axis_name="tok", split_axis=0, concat_axis=0, tiled=True,
        axis_index_groups=peers,
    )
    parts = swap(held.reshape(rows, spatial)).reshape(timesteps, rows // timesteps, spatial)
    sums = pl.pallas_call(
        earlier_kernel,
        out_shape=jax.ShapeDtypeStruct(parts.shape, BF16),
        in_specs=vmem(1),
        out_specs=vmem(1)[0],
        name="earlier",
    )(parts)
    return swap(sums.reshape(rows, spatial)).reshape(held.shape).astype(F32)


def body(
    initial_guess,
    noise_draws,
    drift_state,
    drift_denoise,
    noise_scale,
    modulation,
    embed_weight,
    space_input,
    space_output,
    time_input,
    time_output,
    final_weight,
):
    timesteps = modulation.shape[0]
    devices = lax.axis_size("tok")
    groups = devices // timesteps
    timestep = lax.axis_index("tok") // groups
    leading = timestep == 0
    own = timestep.astype(jnp.int32).reshape(1)
    if groups == 1:
        step = step_fused
    else:
        peers = [[row * groups + block for block in range(groups)] for row in range(timesteps)]
        step = functools.partial(step_split, peers=peers)
    rates = (drift_state, drift_denoise, noise_scale)
    weights = (
        embed_weight, space_input.T, space_output, time_input.T, time_output, final_weight.T
    )

    def iterate(_, held):
        latent = held[0]
        increment, rounded = step(own, rates, latent, noise_draws, modulation, weights)
        before = sum_before(rounded, timesteps, groups)
        return jnp.where(leading, latent, before), before + increment

    return lax.fori_loop(0, ITERS, iterate, (initial_guess, initial_guess))[1]


def solution(mesh):
    rows = P(("group", "tok"), None, None)
    placed = (rows, rows) + (P(),) * 10
    return jax.shard_map(
        body, mesh=mesh, in_specs=placed, out_specs=rows, check_vma=False
    )
```

```python
import functools
import itertools
import math

import jax
import jax.numpy as jnp
from jax import lax
from jax.experimental import pallas as pl
from jax.experimental.pallas import tpu as pltpu
from jax.sharding import PartitionSpec as P

HEADS = 8
ITERS = 2
LANES = 128
ROWS8 = 8
ROWS16 = 16
F32 = jnp.float32
BF16 = jnp.bfloat16


def layer_norm(values):
    center = values - jnp.mean(values, -1, keepdims=True)
    return center * lax.rsqrt(jnp.mean(center * center, -1, keepdims=True) + 1e-06)


def normed_head(values, head_size, scale):
    total = jnp.sum(values * values, 0, keepdims=True)
    return values * (lax.rsqrt(total * (1.0 / head_size) + 1e-06) * scale)


def padded(values, fill, rows):
    extra = rows - values.shape[0]
    return jnp.concatenate(
        [values, jnp.full((extra, values.shape[1]), fill, F32)], 0
    ).astype(BF16)


def on_diagonal(blocks):
    zero = jnp.zeros_like(blocks[0])
    return jnp.concatenate(
        [
            jnp.concatenate([block if at == own else zero for at in range(len(blocks))], 1)
            for own, block in enumerate(blocks)
        ],
        0,
    )


def modulated_norm(values, rows_of, shift, scale):
    return (
        layer_norm(values) * (1.0 + rows_of[scale : scale + 1]) + rows_of[shift : shift + 1]
    ).astype(BF16)


def weave(main, side, main_count, side_count):
    done = 0
    for index, _ in enumerate(main):
        due = -(-(index + 1) * side_count // main_count)
        while done < due:
            next(side, None)
            done += 1
    for _ in side:
        pass


def attention_pieces(normed, input_turned, output_weight, same_position, places, groups, finish):
    query_rows, turned_keys, value_rows, kept, attended, turned_attended = places
    inner, width = output_weight.shape
    tokens = normed.shape[0]
    head_size = inner // HEADS
    deep, tall = query_rows.shape[1], value_rows.shape[1]
    chunk = HEADS // 2
    scale = head_size ** (-0.5) * math.log2(math.e)

    def project(kind):
        rows = input_turned[kind * inner : (kind + 1) * inner]
        return lax.dot_general(
            rows, normed[...], (((1,), (1,)), ((), ())), preferred_element_type=F32
        )

    def keep_projected(kind, packed):
        for head in range(HEADS):
            values = packed[head * head_size : (head + 1) * head_size]
            if kind == 0:
                query_rows[head] = padded(normed_head(values, head_size, scale), 0.0, deep)
            elif kind == 1:
                turned_keys[head] = padded(normed_head(values, head_size, 1.0), 0.0, deep).T
            else:
                value_rows[head] = padded(values, 1.0, tall)

    pairs = [groups[at : at + 2] for at in range(0, len(groups), 2)]

    def over(pair):
        return slice(pair[0].start, pair[-1].stop)

    def score(head, pair):
        return jnp.dot(
            jnp.concatenate([turned_keys[head, group] for group in pair], 1),
            on_diagonal([query_rows[head, :, group] for group in pair]),
            preferred_element_type=F32,
        )

    def keep_scored(head, pair, scores):
        weights = jnp.exp2(scores).astype(BF16)
        if same_position is not None:
            weights = weights * same_position[:, : weights.shape[1]]
        kept[head, :, over(pair)] = weights

    def mix(head, pair):
        return jnp.dot(
            value_rows[head, :, over(pair)],
            on_diagonal([kept[head, :, group] for group in pair]),
            preferred_element_type=F32,
        )

    def keep_mixed(head, pair, mixed):
        rate = 1.0 / mixed[head_size : head_size + ROWS8]
        parts = mixed[:head_size].reshape(head_size // ROWS8, ROWS8, -1) * rate[None]
        first, last = head * head_size, (head + 1) * head_size
        columns = over(pair)
        attended[first:last, columns] = parts.reshape(head_size, -1)
        for at in range(0, inner, LANES):
            stop = min(at + LANES, inner)
            if first < stop <= last:
                turned_attended[columns, at:stop] = attended[at:stop, columns].astype(BF16).T

    def projections(kind):
        return (lambda: project(kind)), (lambda got: keep_projected(kind, got))

    def scorings(head, pair):
        return (lambda: score(head, pair)), (lambda got: keep_scored(head, pair, got))

    def mixings(head, pair):
        return (lambda: mix(head, pair)), (lambda got: keep_mixed(head, pair, got))

    def outputs(at):
        columns = slice(at, min(at + 2 * LANES, width))
        return (
            lambda: jnp.dot(
                turned_attended[...], output_weight[:, columns], preferred_element_type=F32
            )
        ), (lambda got: finish(columns, got))

    every = [(head, pair) for head in range(HEADS) for pair in pairs]
    scored = [scorings(*at) for at in every]
    mixes = [mixings(*at) for at in every]
    first = [projections(0), projections(1), projections(2), scored[0]]
    behind = scored[1:]
    for index, task in enumerate(behind):
        first.append(task)
        if index >= 1:
            first.append(mixes[index - 1])
    first += mixes[len(behind) - 1 :]
    for tasks in (first, [outputs(at) for at in range(0, width, 2 * LANES)]):
        waiting = None
        for issue, use in tasks:
            got = issue()
            if waiting is not None:
                waiting[0](waiting[1])
            waiting = (use, got)
            yield
        waiting[0](waiting[1])
        yield


def main_pieces(groups, width):
    return 3 + HEADS * -(-groups // 2) * 2 + 1 + -(-width // (2 * LANES)) + 1


def run_pipelined(steps, before, main, behind, main_count, before_count, behind_count, ready):
    def one(index, own, last):
        following = jnp.minimum(index + 1, last)
        previous = jnp.maximum(index - 1, 0)
        side = itertools.chain(behind(previous, 1 - own), before(following, 1 - own))
        weave(main(index, own), side, main_count, before_count + behind_count)

    for _ in before(0, 0):
        pass
    ready()
    if steps % 2 == 0:

        @pl.loop(0, steps // 2)
        def _(turn_index):
            one(2 * turn_index, 0, steps - 1)
            one(2 * turn_index + 1, 1, steps - 1)

        for _ in behind(steps - 1, 1):
            pass
    else:
        for index in range(steps):
            one(index, index % 2, steps - 1)
        for _ in behind(steps - 1, (steps - 1) % 2):
            pass


BLOCK = 32


def run_space(latent, embed, rows_of, input_weight, output_weight, out, places, ready):
    frames, _, spatial = latent.shape
    width = embed.shape[1]
    step = groups_of(frames)
    tokens = step * spatial
    normed, base, inner_places = places[:2], places[2:4], places[4:]
    groups = [slice(at, at + spatial) for at in range(0, tokens, spatial)]

    def before(index, own):
        for frame in range(step):
            base[own][groups[frame]] = lax.dot_general(
                latent[index * step + frame].astype(BF16),
                embed[...],
                (((0,), (0,)), ((), ())),
                preferred_element_type=F32,
            )
            yield
        for at in range(0, tokens, BLOCK):
            normed[own][at : at + BLOCK] = modulated_norm(
                base[own][at : at + BLOCK], rows_of, 0, 1
            )
            yield

    def main(index, own):
        def finish(columns, mixed):
            after = base[own][:, columns] + rows_of[2:3, columns] * mixed
            for frame, group in enumerate(groups):
                out[index * step + frame, :, columns] = after[group].astype(out.dtype)

        return attention_pieces(
            normed[own], input_weight, output_weight, None, inner_places, groups, finish
        )

    def behind(index, own):
        return iter(())

    run_pipelined(
        frames // step, before, main, behind, main_pieces(step, width), step + tokens // BLOCK, 0, ready
    )


def run_time(after, rows_of, input_weight, output_weight, final, out, places, ready):
    frames, positions, width = after.shape
    step = groups_of(positions // ROWS8)
    rows = frames * ROWS8
    tokens = step * rows
    normed, settled, inner_places = places[:2], places[2:4], places[4:]
    groups = [slice(at, at + rows) for at in range(0, tokens, rows)]
    same_position = same_position_mask(frames, min(step, 2))

    def eight(index, group):
        at = (index * step + group) * ROWS8
        if not isinstance(at, int):
            at = pl.multiple_of(at, ROWS8)
        return pl.ds(at, ROWS8)

    def before(index, own):
        for group in range(step):
            for at in range(0, rows, BLOCK):
                some = slice(at // ROWS8, (at + BLOCK) // ROWS8)
                hidden = after[some, eight(index, group), :].reshape(BLOCK, width)
                first = groups[group].start + at
                normed[own][first : first + BLOCK] = modulated_norm(hidden, rows_of, 3, 4)
                yield

    def main(index, own):
        def finish(columns, mixed):
            for group in range(step):
                hidden = after[:, eight(index, group), columns].reshape(rows, -1)
                settled[own][groups[group], columns] = (
                    hidden + rows_of[5:6, columns] * mixed[groups[group]]
                )

        return attention_pieces(
            normed[own], input_weight, output_weight, same_position, inner_places, groups, finish
        )

    def behind(index, own):
        for group in range(step):
            for at in range(0, rows, BLOCK):
                first = groups[group].start + at
                last = modulated_norm(settled[own][first : first + BLOCK], rows_of, 6, 7)
                predicted = lax.dot_general(
                    last, final[...], (((1,), (1,)), ((), ())), preferred_element_type=F32
                )
                some = slice(at // ROWS8, (at + BLOCK) // ROWS8)
                out[some, eight(index, group), :] = predicted.reshape(
                    BLOCK // ROWS8, ROWS8, predicted.shape[1]
                )
                yield

    settled[1][...] = jnp.zeros_like(settled[1])
    run_pipelined(
        positions // (step * ROWS8), before, main, behind, main_pieces(step, width),
        tokens // BLOCK, tokens // BLOCK, ready,
    )


def same_position_mask(frames, count):
    shape = (frames * ROWS8, count * frames * ROWS8)
    row = lax.broadcasted_iota(jnp.int32, shape, 0) % ROWS8
    column = lax.broadcasted_iota(jnp.int32, shape, 1) % ROWS8
    return jnp.where(row == column, 1.0, 0.0).astype(BF16)


def groups_of(blocks):
    return next(step for step in (2, 1) if blocks % step == 0)


def fused_kernel(
    timestep, rate_state, rate_denoise, rate_noise, latent, noise, modulation, embed,
    space_in_hbm, space_out_hbm, time_in_hbm, time_out_hbm, final, increment, rounded,
    rows_of, space_in, space_out, time_in, time_out, after, staged, sems, *turned,
):
    own = timestep[0]
    copies = [
        pltpu.make_async_copy(source, target, sems.at[index])
        for index, (source, target) in enumerate(
            (
                (modulation.at[own], rows_of),
                (space_in_hbm, space_in),
                (space_out_hbm, space_out),
                (time_in_hbm, time_in),
                (time_out_hbm, time_out),
            )
        )
    ]
    for copy in copies:
        copy.start()

    def wait_for(some):
        for copy in some:
            copy.wait()

    wait_for(copies[:1])
    run_space(
        latent, embed, rows_of, space_in, space_out, after, turned, lambda: wait_for(copies[1:3])
    )
    run_time(
        after, rows_of, time_in, time_out, final, staged, turned, lambda: wait_for(copies[3:])
    )
    keep = rate_state[own] + jnp.where(own == 0, 1.0, 0.0)
    for frame in range(latent.shape[0]):
        value = (
            keep * latent[frame]
            + rate_denoise[own] * staged[frame].T
            + rate_noise[own] * noise[frame]
        )
        increment[frame] = value
        rounded[frame] = value.astype(BF16)


def space_kernel(latent, rows_of, embed, space_in, space_out, after, *turned):
    run_space(latent, embed, rows_of, space_in, space_out, after, turned, lambda: None)


def time_kernel(after, rows_of, time_in, time_out, final, predicted, *turned):
    run_time(after, rows_of, time_in, time_out, final, predicted, turned, lambda: None)


def vmem(count):
    return [pl.BlockSpec(memory_space=pltpu.VMEM)] * count


PARAMS = dict(compiler_params=pltpu.CompilerParams(vmem_limit_bytes=56 * 2**20))


def turned_scratch(tokens, group_rows, width, inner):
    head_size = inner // HEADS
    deep = -(-head_size // LANES) * LANES
    tall = head_size + ROWS16 - head_size % ROWS16
    return [
        pltpu.VMEM((tokens, width), BF16),
        pltpu.VMEM((tokens, width), BF16),
        pltpu.VMEM((tokens, width), F32),
        pltpu.VMEM((tokens, width), F32),
        pltpu.VMEM((HEADS, deep, tokens), BF16),
        pltpu.VMEM((HEADS, tokens, deep), BF16),
        pltpu.VMEM((HEADS, tall, tokens), BF16),
        pltpu.VMEM((HEADS, group_rows, tokens), BF16),
        pltpu.VMEM((inner, tokens), F32),
        pltpu.VMEM((tokens, inner), BF16),
    ]


def scalars(count):
    return [pl.BlockSpec(memory_space=pltpu.SMEM)] * count


def step_fused(timestep, rates, latent, noise, modulation, weights):
    frames, channels, spatial = latent.shape
    embed, space_in, space_out, time_in, time_out, final = weights
    width = embed.shape[1]
    return pl.pallas_call(
        fused_kernel,
        out_shape=[
            jax.ShapeDtypeStruct(latent.shape, F32),
            jax.ShapeDtypeStruct(latent.shape, BF16),
        ],
        in_specs=scalars(4)
        + vmem(2)
        + [pl.BlockSpec(memory_space=pl.ANY)]
        + vmem(1)
        + [pl.BlockSpec(memory_space=pl.ANY)] * 4
        + vmem(1),
        out_specs=vmem(2),
        scratch_shapes=[
            pltpu.VMEM(modulation.shape[1:], F32),
            pltpu.VMEM(space_in.shape, BF16),
            pltpu.VMEM(space_out.shape, BF16),
            pltpu.VMEM(time_in.shape, BF16),
            pltpu.VMEM(time_out.shape, BF16),
            pltpu.VMEM((frames, spatial, width), F32),
            pltpu.VMEM((frames, spatial, channels), F32),
            pltpu.SemaphoreType.DMA((5,)),
        ]
        + turned_scratch(groups_of(frames) * spatial, spatial, width, space_out.shape[0]),
        name="denoise",
        **PARAMS,
    )(
        timestep, *rates, latent, noise, modulation, embed, space_in, space_out, time_in,
        time_out, final,
    )


def step_split(timestep, rates, latent, noise, modulation, weights, peers):
    frames, channels, spatial = latent.shape
    embed, space_in, space_out, time_in, time_out, final = weights
    width = embed.shape[1]
    own = timestep[0]
    rows_of = lax.dynamic_index_in_dim(modulation, own, 0, keepdims=False)
    after = pl.pallas_call(
        space_kernel,
        out_shape=jax.ShapeDtypeStruct((frames, spatial, width), BF16),
        in_specs=vmem(5),
        out_specs=vmem(1)[0],
        scratch_shapes=turned_scratch(groups_of(frames) * spatial, spatial, width, space_out.shape[0]),
        name="space",
        **PARAMS,
    )(latent, rows_of, embed, space_in, space_out)
    after = lax.all_to_all(
        after, "tok", split_axis=1, concat_axis=0, tiled=True, axis_index_groups=peers
    )
    predicted = pl.pallas_call(
        time_kernel,
        out_shape=jax.ShapeDtypeStruct(after.shape[:2] + (channels,), F32),
        in_specs=vmem(5),
        out_specs=vmem(1)[0],
        scratch_shapes=turned_scratch(
            groups_of(after.shape[1] // ROWS8) * ROWS8 * after.shape[0], ROWS8 * after.shape[0],
            width, time_out.shape[0],
        ),
        name="time",
        **PARAMS,
    )(after.astype(F32), rows_of, time_in, time_out, final)
    predicted = lax.all_to_all(
        predicted, "tok", split_axis=0, concat_axis=1, tiled=True, axis_index_groups=peers
    )
    rate_state, rate_denoise, rate_noise = (rate[own] for rate in rates)
    increment = (
        (rate_state + jnp.where(own == 0, 1.0, 0.0)) * latent
        + rate_denoise * jnp.swapaxes(predicted, 1, 2)
        + rate_noise * noise
    )
    return increment, increment.astype(BF16)


RADIX = 4


def sum_before(values, held, timesteps, groups):
    before = jnp.zeros_like(values)
    reach = 1
    while reach < timesteps:
        arrived = []
        for back in range(reach, min(reach * RADIX, timesteps), reach):
            moves = [
                (step * groups + block, (step + back) * groups + block)
                for step in range(timesteps - back)
                for block in range(groups)
            ]
            arrived.append(lax.ppermute(held, "tok", moves))
        for part in arrived:
            before = before + part.astype(F32)
        held = (values + before).astype(BF16)
        reach *= RADIX
    return before


def body(
    initial_guess,
    noise_draws,
    drift_state,
    drift_denoise,
    noise_scale,
    modulation,
    embed_weight,
    space_input,
    space_output,
    time_input,
    time_output,
    final_weight,
):
    timesteps = modulation.shape[0]
    devices = lax.axis_size("tok")
    groups = devices // timesteps
    timestep = lax.axis_index("tok") // groups
    leading = timestep == 0
    own = timestep.astype(jnp.int32).reshape(1)
    if groups == 1:
        step = step_fused
    else:
        peers = [[row * groups + block for block in range(groups)] for row in range(timesteps)]
        step = functools.partial(step_split, peers=peers)
    rates = (drift_state, drift_denoise, noise_scale)
    weights = (
        embed_weight, space_input.T, space_output, time_input.T, time_output, final_weight.T
    )
    latent = initial_guess
    result = initial_guess
    for _ in range(ITERS):
        increment, rounded = step(own, rates, latent, noise_draws, modulation, weights)
        before = sum_before(increment, rounded, timesteps, groups)
        result = before + increment
        latent = jnp.where(leading, latent, before)
    return result


def solution(mesh):
    rows = P(("group", "tok"), None, None)
    placed = (rows, rows) + (P(),) * 10
    return jax.shard_map(
        body, mesh=mesh, in_specs=placed, out_specs=rows, check_vma=False
    )
```

```python
import functools
import itertools
import math

import jax
import jax.numpy as jnp
from jax import lax
from jax.experimental import pallas as pl
from jax.experimental.pallas import tpu as pltpu
from jax.sharding import PartitionSpec as P

HEADS = 8
ITERS = 2
LANES = 128
ROWS8 = 8
ROWS16 = 16
F32 = jnp.float32
BF16 = jnp.bfloat16


def layer_norm(values):
    center = values - jnp.mean(values, -1, keepdims=True)
    return center * lax.rsqrt(jnp.mean(center * center, -1, keepdims=True) + 1e-06)


def normed_head(values, head_size, scale):
    total = jnp.sum(values * values, 0, keepdims=True)
    return values * (lax.rsqrt(total * (1.0 / head_size) + 1e-06) * scale)


def padded(values, fill, rows):
    extra = rows - values.shape[0]
    return jnp.concatenate(
        [values, jnp.full((extra, values.shape[1]), fill, F32)], 0
    ).astype(BF16)


def on_diagonal(blocks):
    zero = jnp.zeros_like(blocks[0])
    return jnp.concatenate(
        [
            jnp.concatenate([block if at == own else zero for at in range(len(blocks))], 1)
            for own, block in enumerate(blocks)
        ],
        0,
    )


def modulated_norm(values, rows_of, shift, scale):
    return (
        layer_norm(values) * (1.0 + rows_of[scale : scale + 1]) + rows_of[shift : shift + 1]
    ).astype(BF16)


def weave(main, side, main_count, side_count):
    done = 0
    for index, _ in enumerate(main):
        due = -(-(index + 1) * side_count // main_count)
        while done < due:
            next(side, None)
            done += 1
    for _ in side:
        pass


def attention_pieces(normed, input_turned, output_weight, same_position, places, groups, finish):
    query_rows, turned_keys, value_rows, kept, attended, turned_attended = places
    inner, width = output_weight.shape
    tokens = normed.shape[0]
    head_size = inner // HEADS
    deep, tall = query_rows.shape[1], value_rows.shape[1]
    chunk = HEADS // 2
    scale = head_size ** (-0.5) * math.log2(math.e)

    half_heads = HEADS // 2

    def project(kind, half):
        at = kind * inner + half * half_heads * head_size
        rows = input_turned[at : at + half_heads * head_size]
        return lax.dot_general(
            rows, normed[...], (((1,), (1,)), ((), ())), preferred_element_type=F32
        )

    def keep_projected(kind, half, packed):
        for index in range(half_heads):
            head = half * half_heads + index
            values = packed[index * head_size : (index + 1) * head_size]
            if kind == 0:
                query_rows[head] = padded(normed_head(values, head_size, scale), 0.0, deep)
            elif kind == 1:
                turned_keys[head] = padded(normed_head(values, head_size, 1.0), 0.0, deep).T
            else:
                value_rows[head] = padded(values, 1.0, tall)

    pairs = [groups[at : at + 2] for at in range(0, len(groups), 2)]

    def over(pair):
        return slice(pair[0].start, pair[-1].stop)

    def score(head, pair):
        return jnp.dot(
            jnp.concatenate([turned_keys[head, group] for group in pair], 1),
            on_diagonal([query_rows[head, :, group] for group in pair]),
            preferred_element_type=F32,
        )

    def keep_scored(head, pair, scores):
        weights = jnp.exp2(scores).astype(BF16)
        if same_position is not None:
            weights = weights * same_position[:, : weights.shape[1]]
        kept[head, :, over(pair)] = weights

    def mix(head, pair):
        return jnp.dot(
            value_rows[head, :, over(pair)],
            on_diagonal([kept[head, :, group] for group in pair]),
            preferred_element_type=F32,
        )

    def keep_mixed(head, pair, mixed):
        rate = 1.0 / mixed[head_size : head_size + ROWS8]
        parts = mixed[:head_size].reshape(head_size // ROWS8, ROWS8, -1) * rate[None]
        first, last = head * head_size, (head + 1) * head_size
        columns = over(pair)
        attended[first:last, columns] = parts.reshape(head_size, -1)
        for at in range(0, inner, LANES):
            stop = min(at + LANES, inner)
            if first < stop <= last:
                turned_attended[columns, at:stop] = attended[at:stop, columns].astype(BF16).T

    def projections(kind, half):
        return (lambda: project(kind, half)), (lambda got: keep_projected(kind, half, got))

    def scorings(head, pair):
        return (lambda: score(head, pair)), (lambda got: keep_scored(head, pair, got))

    def mixings(head, pair):
        return (lambda: mix(head, pair)), (lambda got: keep_mixed(head, pair, got))

    def outputs(at):
        columns = slice(at, min(at + 2 * LANES, width))
        return (
            lambda: jnp.dot(
                turned_attended[...], output_weight[:, columns], preferred_element_type=F32
            )
        ), (lambda got: finish(columns, got))

    every = [(head, pair) for head in range(HEADS) for pair in pairs]
    scored = [scorings(*at) for at in every]
    mixes = [mixings(*at) for at in every]
    first = [projections(0, 0), projections(1, 0), projections(0, 1)]
    for task, later in zip(scored, (projections(1, 1), projections(2, 0), projections(2, 1))):
        first += [task, later]
    behind = scored[3:]
    for index, task in enumerate(behind):
        first.append(task)
        if index >= 1:
            first.append(mixes[index - 1])
    first += mixes[len(behind) - 1 :]
    for tasks in (first, [outputs(at) for at in range(0, width, 2 * LANES)]):
        waiting = None
        for issue, use in tasks:
            got = issue()
            if waiting is not None:
                waiting[0](waiting[1])
            waiting = (use, got)
            yield
        waiting[0](waiting[1])
        yield


def main_pieces(groups, width):
    return 6 + HEADS * -(-groups // 2) * 2 + 1 + -(-width // (2 * LANES)) + 1


def run_pipelined(steps, before, main, behind, main_count, before_count, behind_count, ready):
    def one(index, own, last):
        following = jnp.minimum(index + 1, last)
        previous = jnp.maximum(index - 1, 0)
        side = itertools.chain(behind(previous, 1 - own), before(following, 1 - own))
        weave(main(index, own), side, main_count, before_count + behind_count)

    for _ in before(0, 0):
        pass
    ready()
    if steps % 2 == 0:

        @pl.loop(0, steps // 2)
        def _(turn_index):
            one(2 * turn_index, 0, steps - 1)
            one(2 * turn_index + 1, 1, steps - 1)

        for _ in behind(steps - 1, 1):
            pass
    else:
        for index in range(steps):
            one(index, index % 2, steps - 1)
        for _ in behind(steps - 1, (steps - 1) % 2):
            pass


BLOCK = 32


def run_space(latent, embed, rows_of, input_weight, output_weight, out, places, ready):
    frames, _, spatial = latent.shape
    width = embed.shape[1]
    step = groups_of(frames)
    tokens = step * spatial
    normed, base, inner_places = places[:2], places[2:4], places[4:]
    groups = [slice(at, at + spatial) for at in range(0, tokens, spatial)]

    def before(index, own):
        for frame in range(step):
            base[own][groups[frame]] = lax.dot_general(
                latent[index * step + frame].astype(BF16),
                embed[...],
                (((0,), (0,)), ((), ())),
                preferred_element_type=F32,
            )
            yield
        for at in range(0, tokens, BLOCK):
            normed[own][at : at + BLOCK] = modulated_norm(
                base[own][at : at + BLOCK], rows_of, 0, 1
            )
            yield

    def main(index, own):
        def finish(columns, mixed):
            after = base[own][:, columns] + rows_of[2:3, columns] * mixed
            for frame, group in enumerate(groups):
                out[index * step + frame, :, columns] = after[group].astype(out.dtype)

        return attention_pieces(
            normed[own], input_weight, output_weight, None, inner_places, groups, finish
        )

    def behind(index, own):
        return iter(())

    run_pipelined(
        frames // step, before, main, behind, main_pieces(step, width), step + tokens // BLOCK, 0, ready
    )


def run_time(after, rows_of, input_weight, output_weight, final, out, places, ready):
    frames, positions, width = after.shape
    step = groups_of(positions // ROWS8)
    rows = frames * ROWS8
    tokens = step * rows
    normed, settled, inner_places = places[:2], places[2:4], places[4:]
    groups = [slice(at, at + rows) for at in range(0, tokens, rows)]
    same_position = same_position_mask(frames, min(step, 2))

    def eight(index, group):
        at = (index * step + group) * ROWS8
        if not isinstance(at, int):
            at = pl.multiple_of(at, ROWS8)
        return pl.ds(at, ROWS8)

    def before(index, own):
        for group in range(step):
            for at in range(0, rows, BLOCK):
                some = slice(at // ROWS8, (at + BLOCK) // ROWS8)
                hidden = after[some, eight(index, group), :].reshape(BLOCK, width)
                first = groups[group].start + at
                normed[own][first : first + BLOCK] = modulated_norm(hidden, rows_of, 3, 4)
                yield

    def main(index, own):
        def finish(columns, mixed):
            for group in range(step):
                hidden = after[:, eight(index, group), columns].reshape(rows, -1)
                settled[own][groups[group], columns] = (
                    hidden + rows_of[5:6, columns] * mixed[groups[group]]
                )

        return attention_pieces(
            normed[own], input_weight, output_weight, same_position, inner_places, groups, finish
        )

    def behind(index, own):
        for group in range(step):
            for at in range(0, rows, BLOCK):
                first = groups[group].start + at
                last = modulated_norm(settled[own][first : first + BLOCK], rows_of, 6, 7)
                predicted = lax.dot_general(
                    last, final[...], (((1,), (1,)), ((), ())), preferred_element_type=F32
                )
                some = slice(at // ROWS8, (at + BLOCK) // ROWS8)
                out[some, eight(index, group), :] = predicted.reshape(
                    BLOCK // ROWS8, ROWS8, predicted.shape[1]
                )
                yield

    settled[1][...] = jnp.zeros_like(settled[1])
    run_pipelined(
        positions // (step * ROWS8), before, main, behind, main_pieces(step, width),
        tokens // BLOCK, tokens // BLOCK, ready,
    )


def same_position_mask(frames, count):
    shape = (frames * ROWS8, count * frames * ROWS8)
    row = lax.broadcasted_iota(jnp.int32, shape, 0) % ROWS8
    column = lax.broadcasted_iota(jnp.int32, shape, 1) % ROWS8
    return jnp.where(row == column, 1.0, 0.0).astype(BF16)


def groups_of(blocks):
    return next(step for step in (4, 2, 1) if blocks % step == 0)


def fused_kernel(
    timestep, rate_state, rate_denoise, rate_noise, latent, noise, modulation, embed,
    space_in_hbm, space_out_hbm, time_in_hbm, time_out_hbm, final, increment, rounded,
    rows_of, space_in, space_out, time_in, time_out, after, staged, sems, *turned,
):
    own = timestep[0]
    copies = [
        pltpu.make_async_copy(source, target, sems.at[index])
        for index, (source, target) in enumerate(
            (
                (modulation.at[own], rows_of),
                (space_in_hbm, space_in),
                (space_out_hbm, space_out),
                (time_in_hbm, time_in),
                (time_out_hbm, time_out),
            )
        )
    ]
    for copy in copies:
        copy.start()

    def wait_for(some):
        for copy in some:
            copy.wait()

    wait_for(copies[:1])
    run_space(
        latent, embed, rows_of, space_in, space_out, after, turned, lambda: wait_for(copies[1:3])
    )
    run_time(
        after, rows_of, time_in, time_out, final, staged, turned, lambda: wait_for(copies[3:])
    )
    keep = rate_state[own] + jnp.where(own == 0, 1.0, 0.0)
    for frame in range(latent.shape[0]):
        value = (
            keep * latent[frame]
            + rate_denoise[own] * staged[frame].T
            + rate_noise[own] * noise[frame]
        )
        increment[frame] = value
        rounded[frame] = value.astype(BF16)


def space_kernel(latent, rows_of, embed, space_in, space_out, after, *turned):
    run_space(latent, embed, rows_of, space_in, space_out, after, turned, lambda: None)


def time_kernel(after, rows_of, time_in, time_out, final, predicted, *turned):
    run_time(after, rows_of, time_in, time_out, final, predicted, turned, lambda: None)


def vmem(count):
    return [pl.BlockSpec(memory_space=pltpu.VMEM)] * count


PARAMS = dict(compiler_params=pltpu.CompilerParams(vmem_limit_bytes=56 * 2**20))


def turned_scratch(tokens, group_rows, width, inner):
    head_size = inner // HEADS
    deep = -(-head_size // LANES) * LANES
    tall = head_size + ROWS16 - head_size % ROWS16
    return [
        pltpu.VMEM((tokens, width), BF16),
        pltpu.VMEM((tokens, width), BF16),
        pltpu.VMEM((tokens, width), F32),
        pltpu.VMEM((tokens, width), F32),
        pltpu.VMEM((HEADS, deep, tokens), BF16),
        pltpu.VMEM((HEADS, tokens, deep), BF16),
        pltpu.VMEM((HEADS, tall, tokens), BF16),
        pltpu.VMEM((HEADS, group_rows, tokens), BF16),
        pltpu.VMEM((inner, tokens), F32),
        pltpu.VMEM((tokens, inner), BF16),
    ]


def scalars(count):
    return [pl.BlockSpec(memory_space=pltpu.SMEM)] * count


def step_fused(timestep, rates, latent, noise, modulation, weights):
    frames, channels, spatial = latent.shape
    embed, space_in, space_out, time_in, time_out, final = weights
    width = embed.shape[1]
    return pl.pallas_call(
        fused_kernel,
        out_shape=[
            jax.ShapeDtypeStruct(latent.shape, F32),
            jax.ShapeDtypeStruct(latent.shape, BF16),
        ],
        in_specs=scalars(4)
        + vmem(2)
        + [pl.BlockSpec(memory_space=pl.ANY)]
        + vmem(1)
        + [pl.BlockSpec(memory_space=pl.ANY)] * 4
        + vmem(1),
        out_specs=vmem(2),
        scratch_shapes=[
            pltpu.VMEM(modulation.shape[1:], F32),
            pltpu.VMEM(space_in.shape, BF16),
            pltpu.VMEM(space_out.shape, BF16),
            pltpu.VMEM(time_in.shape, BF16),
            pltpu.VMEM(time_out.shape, BF16),
            pltpu.VMEM((frames, spatial, width), F32),
            pltpu.VMEM((frames, spatial, channels), F32),
            pltpu.SemaphoreType.DMA((5,)),
        ]
        + turned_scratch(groups_of(frames) * spatial, spatial, width, space_out.shape[0]),
        name="denoise",
        **PARAMS,
    )(
        timestep, *rates, latent, noise, modulation, embed, space_in, space_out, time_in,
        time_out, final,
    )


def step_split(timestep, rates, latent, noise, modulation, weights, peers):
    frames, channels, spatial = latent.shape
    embed, space_in, space_out, time_in, time_out, final = weights
    width = embed.shape[1]
    own = timestep[0]
    rows_of = lax.dynamic_index_in_dim(modulation, own, 0, keepdims=False)
    after = pl.pallas_call(
        space_kernel,
        out_shape=jax.ShapeDtypeStruct((frames, spatial, width), BF16),
        in_specs=vmem(5),
        out_specs=vmem(1)[0],
        scratch_shapes=turned_scratch(groups_of(frames) * spatial, spatial, width, space_out.shape[0]),
        name="space",
        **PARAMS,
    )(latent, rows_of, embed, space_in, space_out)
    after = lax.all_to_all(
        after, "tok", split_axis=1, concat_axis=0, tiled=True, axis_index_groups=peers
    )
    predicted = pl.pallas_call(
        time_kernel,
        out_shape=jax.ShapeDtypeStruct(after.shape[:2] + (channels,), F32),
        in_specs=vmem(5),
        out_specs=vmem(1)[0],
        scratch_shapes=turned_scratch(
            groups_of(after.shape[1] // ROWS8) * ROWS8 * after.shape[0], ROWS8 * after.shape[0],
            width, time_out.shape[0],
        ),
        name="time",
        **PARAMS,
    )(after.astype(F32), rows_of, time_in, time_out, final)
    predicted = lax.all_to_all(
        predicted, "tok", split_axis=0, concat_axis=1, tiled=True, axis_index_groups=peers
    )
    rate_state, rate_denoise, rate_noise = (rate[own] for rate in rates)
    increment = (
        (rate_state + jnp.where(own == 0, 1.0, 0.0)) * latent
        + rate_denoise * jnp.swapaxes(predicted, 1, 2)
        + rate_noise * noise
    )
    return increment, increment.astype(BF16)


RADIX = 4


def sum_before(values, held, timesteps, groups):
    before = jnp.zeros_like(values)
    reach = 1
    while reach < timesteps:
        arrived = []
        for back in range(reach, min(reach * RADIX, timesteps), reach):
            moves = [
                (step * groups + block, (step + back) * groups + block)
                for step in range(timesteps - back)
                for block in range(groups)
            ]
            arrived.append(lax.ppermute(held, "tok", moves))
        for part in arrived:
            before = before + part.astype(F32)
        held = (values + before).astype(BF16)
        reach *= RADIX
    return before


def body(
    initial_guess,
    noise_draws,
    drift_state,
    drift_denoise,
    noise_scale,
    modulation,
    embed_weight,
    space_input,
    space_output,
    time_input,
    time_output,
    final_weight,
):
    timesteps = modulation.shape[0]
    devices = lax.axis_size("tok")
    groups = devices // timesteps
    timestep = lax.axis_index("tok") // groups
    leading = timestep == 0
    own = timestep.astype(jnp.int32).reshape(1)
    if groups == 1:
        step = step_fused
    else:
        peers = [[row * groups + block for block in range(groups)] for row in range(timesteps)]
        step = functools.partial(step_split, peers=peers)
    rates = (drift_state, drift_denoise, noise_scale)
    weights = (
        embed_weight, space_input.T, space_output, time_input.T, time_output, final_weight.T
    )

    def iterate(_, held):
        latent = held[0]
        increment, rounded = step(own, rates, latent, noise_draws, modulation, weights)
        before = sum_before(increment, rounded, timesteps, groups)
        return jnp.where(leading, latent, before), before + increment

    return lax.fori_loop(0, ITERS, iterate, (initial_guess, initial_guess))[1]


def solution(mesh):
    rows = P(("group", "tok"), None, None)
    placed = (rows, rows) + (P(),) * 10
    return jax.shard_map(
        body, mesh=mesh, in_specs=placed, out_specs=rows, check_vma=False
    )
```

```python
import functools
import itertools
import math

import jax
import jax.numpy as jnp
from jax import lax
from jax.experimental import pallas as pl
from jax.experimental.pallas import tpu as pltpu
from jax.sharding import PartitionSpec as P

HEADS = 8
ITERS = 2
LANES = 128
ROWS8 = 8
ROWS16 = 16
F32 = jnp.float32
BF16 = jnp.bfloat16


def layer_norm(values):
    center = values - jnp.mean(values, -1, keepdims=True)
    return center * lax.rsqrt(jnp.mean(center * center, -1, keepdims=True) + 1e-06)


def normed_head(values, head_size, scale):
    total = jnp.sum(values * values, 0, keepdims=True)
    return values * (lax.rsqrt(total * (1.0 / head_size) + 1e-06) * scale)


def padded(values, fill, rows):
    extra = rows - values.shape[0]
    return jnp.concatenate(
        [values, jnp.full((extra, values.shape[1]), fill, F32)], 0
    ).astype(BF16)


def on_diagonal(blocks):
    zero = jnp.zeros_like(blocks[0])
    return jnp.concatenate(
        [
            jnp.concatenate([block if at == own else zero for at in range(len(blocks))], 1)
            for own, block in enumerate(blocks)
        ],
        0,
    )


def modulated_norm(values, rows_of, shift, scale):
    return (
        layer_norm(values) * (1.0 + rows_of[scale : scale + 1]) + rows_of[shift : shift + 1]
    ).astype(BF16)


def weave(main, side, main_count, side_count):
    done = 0
    for index, _ in enumerate(main):
        due = -(-(index + 1) * side_count // main_count)
        while done < due:
            next(side, None)
            done += 1
    for _ in side:
        pass


def attention_pieces(normed, input_turned, output_weight, same_position, places, groups, finish):
    query_rows, turned_keys, value_rows, kept, attended, turned_attended = places
    inner, width = output_weight.shape
    tokens = normed.shape[0]
    head_size = inner // HEADS
    deep, tall = query_rows.shape[1], value_rows.shape[1]
    chunk = HEADS // 2
    scale = head_size ** (-0.5) * math.log2(math.e)

    def project(kind):
        rows = input_turned[kind * inner : (kind + 1) * inner]
        return lax.dot_general(
            rows, normed[...], (((1,), (1,)), ((), ())), preferred_element_type=F32
        )

    def keep_projected(kind, packed):
        for head in range(HEADS):
            values = packed[head * head_size : (head + 1) * head_size]
            if kind == 0:
                query_rows[head] = padded(normed_head(values, head_size, scale), 0.0, deep)
            elif kind == 1:
                turned_keys[head] = padded(normed_head(values, head_size, 1.0), 0.0, deep).T
            else:
                value_rows[head] = padded(values, 1.0, tall)

    pairs = [groups[at : at + 2] for at in range(0, len(groups), 2)]

    def over(pair):
        return slice(pair[0].start, pair[-1].stop)

    def score(head, pair):
        return jnp.dot(
            jnp.concatenate([turned_keys[head, group] for group in pair], 1),
            on_diagonal([query_rows[head, :, group] for group in pair]),
            preferred_element_type=F32,
        )

    def keep_scored(head, pair, scores):
        weights = jnp.exp2(scores).astype(BF16)
        if same_position is not None:
            weights = weights * same_position[:, : weights.shape[1]]
        kept[head, :, over(pair)] = weights

    def mix(head, pair):
        return jnp.dot(
            value_rows[head, :, over(pair)],
            on_diagonal([kept[head, :, group] for group in pair]),
            preferred_element_type=F32,
        )

    def keep_mixed(head, pair, mixed):
        rate = 1.0 / mixed[head_size : head_size + ROWS8]
        parts = mixed[:head_size].reshape(head_size // ROWS8, ROWS8, -1) * rate[None]
        first, last = head * head_size, (head + 1) * head_size
        columns = over(pair)
        attended[first:last, columns] = parts.reshape(head_size, -1)
        for at in range(0, inner, LANES):
            stop = min(at + LANES, inner)
            if first < stop <= last:
                turned_attended[columns, at:stop] = attended[at:stop, columns].astype(BF16).T

    def projections(kind):
        return (lambda: project(kind)), (lambda got: keep_projected(kind, got))

    def scorings(head, pair):
        return (lambda: score(head, pair)), (lambda got: keep_scored(head, pair, got))

    def mixings(head, pair):
        return (lambda: mix(head, pair)), (lambda got: keep_mixed(head, pair, got))

    def outputs(at):
        columns = slice(at, min(at + 2 * LANES, width))
        return (
            lambda: jnp.dot(
                turned_attended[...], output_weight[:, columns], preferred_element_type=F32
            )
        ), (lambda got: finish(columns, got))

    every = [(head, pair) for head in range(HEADS) for pair in pairs]
    scored = [scorings(*at) for at in every]
    mixes = [mixings(*at) for at in every]
    first = [projections(0), projections(1), projections(2), scored[0]]
    behind = scored[1:]
    for index, task in enumerate(behind):
        first.append(task)
        if index >= 1:
            first.append(mixes[index - 1])
    first += mixes[len(behind) - 1 :]
    for tasks in (first, [outputs(at) for at in range(0, width, 2 * LANES)]):
        waiting = None
        for issue, use in tasks:
            got = issue()
            if waiting is not None:
                waiting[0](waiting[1])
            waiting = (use, got)
            yield
        waiting[0](waiting[1])
        yield


def main_pieces(groups, width):
    return 3 + HEADS * -(-groups // 2) * 2 + 1 + -(-width // (2 * LANES)) + 1


def run_pipelined(steps, before, main, behind, main_count, before_count, behind_count, ready):
    def one(index, own, last):
        following = jnp.minimum(index + 1, last)
        previous = jnp.maximum(index - 1, 0)
        side = itertools.chain(behind(previous, 1 - own), before(following, 1 - own))
        weave(main(index, own), side, main_count, before_count + behind_count)

    for _ in before(0, 0):
        pass
    ready()
    if steps % 2 == 0:

        @pl.loop(0, steps // 2)
        def _(turn_index):
            one(2 * turn_index, 0, steps - 1)
            one(2 * turn_index + 1, 1, steps - 1)

        for _ in behind(steps - 1, 1):
            pass
    else:
        for index in range(steps):
            one(index, index % 2, steps - 1)
        for _ in behind(steps - 1, (steps - 1) % 2):
            pass


BLOCK = 16


def run_space(latent, embed, rows_of, input_weight, output_weight, out, places, ready):
    frames, _, spatial = latent.shape
    width = embed.shape[1]
    step = groups_of(frames)
    tokens = step * spatial
    normed, base, inner_places = places[:2], places[2:4], places[5:]
    groups = [slice(at, at + spatial) for at in range(0, tokens, spatial)]

    def before(index, own):
        for frame in range(step):
            base[own][groups[frame]] = lax.dot_general(
                latent[index * step + frame].astype(BF16),
                embed[...],
                (((0,), (0,)), ((), ())),
                preferred_element_type=F32,
            )
            yield
        for at in range(0, tokens, BLOCK):
            normed[own][at : at + BLOCK] = modulated_norm(
                base[own][at : at + BLOCK], rows_of, 0, 1
            )
            yield

    def main(index, own):
        def finish(columns, mixed):
            after = base[own][:, columns] + rows_of[2:3, columns] * mixed
            for frame, group in enumerate(groups):
                out[index * step + frame, :, columns] = after[group].astype(out.dtype)

        return attention_pieces(
            normed[own], input_weight, output_weight, None, inner_places, groups, finish
        )

    def behind(index, own):
        return iter(())

    run_pipelined(
        frames // step, before, main, behind, main_pieces(step, width), step + tokens // BLOCK, 0, ready
    )


def run_time(after, rows_of, input_weight, output_weight, final, out, places, ready):
    frames, positions, width = after.shape
    step = groups_of(positions // ROWS8)
    rows = frames * ROWS8
    tokens = step * rows
    normed, settled, last, inner_places = places[:2], places[2:4], places[4], places[5:]
    groups = [slice(at, at + rows) for at in range(0, tokens, rows)]
    same_position = same_position_mask(frames, min(step, 2))

    def eight(index, group):
        at = (index * step + group) * ROWS8
        if not isinstance(at, int):
            at = pl.multiple_of(at, ROWS8)
        return pl.ds(at, ROWS8)

    def before(index, own):
        for group in range(step):
            for at in range(0, rows, BLOCK):
                some = slice(at // ROWS8, (at + BLOCK) // ROWS8)
                hidden = after[some, eight(index, group), :].reshape(BLOCK, width)
                first = groups[group].start + at
                normed[own][first : first + BLOCK] = modulated_norm(hidden, rows_of, 3, 4)
                yield

    def main(index, own):
        def finish(columns, mixed):
            for group in range(step):
                hidden = after[:, eight(index, group), columns].reshape(rows, -1)
                settled[own][groups[group], columns] = (
                    hidden + rows_of[5:6, columns] * mixed[groups[group]]
                )

        return attention_pieces(
            normed[own], input_weight, output_weight, same_position, inner_places, groups, finish
        )

    def behind(index, own):
        for at in range(0, tokens, BLOCK):
            last[at : at + BLOCK] = modulated_norm(settled[own][at : at + BLOCK], rows_of, 6, 7)
            yield
        predicted = lax.dot_general(
            final[...], last[...], (((1,), (1,)), ((), ())), preferred_element_type=F32
        )
        for group in range(step):
            part = predicted[:, groups[group]].T
            out[:, eight(index, group), :] = part.reshape(frames, ROWS8, part.shape[1])
        yield

    settled[1][...] = jnp.zeros_like(settled[1])
    run_pipelined(
        positions // (step * ROWS8), before, main, behind, main_pieces(step, width),
        tokens // BLOCK, tokens // BLOCK + 1, ready,
    )


def same_position_mask(frames, count):
    shape = (frames * ROWS8, count * frames * ROWS8)
    row = lax.broadcasted_iota(jnp.int32, shape, 0) % ROWS8
    column = lax.broadcasted_iota(jnp.int32, shape, 1) % ROWS8
    return jnp.where(row == column, 1.0, 0.0).astype(BF16)


def groups_of(blocks):
    return next(step for step in (4, 2, 1) if blocks % step == 0)


def fused_kernel(
    timestep, rate_state, rate_denoise, rate_noise, latent, noise, modulation, embed,
    space_in_hbm, space_out_hbm, time_in_hbm, time_out_hbm, final, increment, rounded,
    rows_of, space_in, space_out, time_in, time_out, after, staged, sems, *turned,
):
    own = timestep[0]
    copies = [
        pltpu.make_async_copy(source, target, sems.at[index])
        for index, (source, target) in enumerate(
            (
                (modulation.at[own], rows_of),
                (space_in_hbm, space_in),
                (space_out_hbm, space_out),
                (time_in_hbm, time_in),
                (time_out_hbm, time_out),
            )
        )
    ]
    for copy in copies:
        copy.start()

    def wait_for(some):
        for copy in some:
            copy.wait()

    wait_for(copies[:1])
    run_space(
        latent, embed, rows_of, space_in, space_out, after, turned, lambda: wait_for(copies[1:3])
    )
    run_time(
        after, rows_of, time_in, time_out, final, staged, turned, lambda: wait_for(copies[3:])
    )
    keep = rate_state[own] + jnp.where(own == 0, 1.0, 0.0)
    for frame in range(latent.shape[0]):
        value = (
            keep * latent[frame]
            + rate_denoise[own] * staged[frame].T
            + rate_noise[own] * noise[frame]
        )
        increment[frame] = value
        rounded[frame] = value.astype(BF16)


def space_kernel(latent, rows_of, embed, space_in, space_out, after, *turned):
    run_space(latent, embed, rows_of, space_in, space_out, after, turned, lambda: None)


def time_kernel(after, rows_of, time_in, time_out, final, predicted, *turned):
    run_time(after, rows_of, time_in, time_out, final, predicted, turned, lambda: None)


def vmem(count):
    return [pl.BlockSpec(memory_space=pltpu.VMEM)] * count


PARAMS = dict(compiler_params=pltpu.CompilerParams(vmem_limit_bytes=56 * 2**20))


def turned_scratch(tokens, group_rows, width, inner):
    head_size = inner // HEADS
    deep = -(-head_size // LANES) * LANES
    tall = head_size + ROWS16 - head_size % ROWS16
    return [
        pltpu.VMEM((tokens, width), BF16),
        pltpu.VMEM((tokens, width), BF16),
        pltpu.VMEM((tokens, width), F32),
        pltpu.VMEM((tokens, width), F32),
        pltpu.VMEM((tokens, width), BF16),
        pltpu.VMEM((HEADS, deep, tokens), BF16),
        pltpu.VMEM((HEADS, tokens, deep), BF16),
        pltpu.VMEM((HEADS, tall, tokens), BF16),
        pltpu.VMEM((HEADS, group_rows, tokens), BF16),
        pltpu.VMEM((inner, tokens), F32),
        pltpu.VMEM((tokens, inner), BF16),
    ]


def scalars(count):
    return [pl.BlockSpec(memory_space=pltpu.SMEM)] * count


def step_fused(timestep, rates, latent, noise, modulation, weights):
    frames, channels, spatial = latent.shape
    embed, space_in, space_out, time_in, time_out, final = weights
    width = embed.shape[1]
    return pl.pallas_call(
        fused_kernel,
        out_shape=[
            jax.ShapeDtypeStruct(latent.shape, F32),
            jax.ShapeDtypeStruct(latent.shape, BF16),
        ],
        in_specs=scalars(4)
        + vmem(2)
        + [pl.BlockSpec(memory_space=pl.ANY)]
        + vmem(1)
        + [pl.BlockSpec(memory_space=pl.ANY)] * 4
        + vmem(1),
        out_specs=vmem(2),
        scratch_shapes=[
            pltpu.VMEM(modulation.shape[1:], F32),
            pltpu.VMEM(space_in.shape, BF16),
            pltpu.VMEM(space_out.shape, BF16),
            pltpu.VMEM(time_in.shape, BF16),
            pltpu.VMEM(time_out.shape, BF16),
            pltpu.VMEM((frames, spatial, width), F32),
            pltpu.VMEM((frames, spatial, channels), F32),
            pltpu.SemaphoreType.DMA((5,)),
        ]
        + turned_scratch(groups_of(frames) * spatial, spatial, width, space_out.shape[0]),
        name="denoise",
        **PARAMS,
    )(
        timestep, *rates, latent, noise, modulation, embed, space_in, space_out, time_in,
        time_out, final,
    )


def step_split(timestep, rates, latent, noise, modulation, weights, peers):
    frames, channels, spatial = latent.shape
    embed, space_in, space_out, time_in, time_out, final = weights
    width = embed.shape[1]
    own = timestep[0]
    rows_of = lax.dynamic_index_in_dim(modulation, own, 0, keepdims=False)
    after = pl.pallas_call(
        space_kernel,
        out_shape=jax.ShapeDtypeStruct((frames, spatial, width), BF16),
        in_specs=vmem(5),
        out_specs=vmem(1)[0],
        scratch_shapes=turned_scratch(groups_of(frames) * spatial, spatial, width, space_out.shape[0]),
        name="space",
        **PARAMS,
    )(latent, rows_of, embed, space_in, space_out)
    after = lax.all_to_all(
        after, "tok", split_axis=1, concat_axis=0, tiled=True, axis_index_groups=peers
    )
    predicted = pl.pallas_call(
        time_kernel,
        out_shape=jax.ShapeDtypeStruct(after.shape[:2] + (channels,), F32),
        in_specs=vmem(5),
        out_specs=vmem(1)[0],
        scratch_shapes=turned_scratch(
            groups_of(after.shape[1] // ROWS8) * ROWS8 * after.shape[0], ROWS8 * after.shape[0],
            width, time_out.shape[0],
        ),
        name="time",
        **PARAMS,
    )(after.astype(F32), rows_of, time_in, time_out, final)
    predicted = lax.all_to_all(
        predicted, "tok", split_axis=0, concat_axis=1, tiled=True, axis_index_groups=peers
    )
    rate_state, rate_denoise, rate_noise = (rate[own] for rate in rates)
    increment = (
        (rate_state + jnp.where(own == 0, 1.0, 0.0)) * latent
        + rate_denoise * jnp.swapaxes(predicted, 1, 2)
        + rate_noise * noise
    )
    return increment, increment.astype(BF16)


def earlier_kernel(parts, sums):
    total = jnp.zeros(parts.shape[1:], F32)
    for step in range(parts.shape[0]):
        sums[step] = total.astype(BF16)
        total = total + parts[step].astype(F32)


def sum_before(held, timesteps, groups):
    frames, channels, spatial = held.shape
    rows = frames * channels
    peers = None
    if groups > 1:
        peers = [[step * groups + block for step in range(timesteps)] for block in range(groups)]
    swap = functools.partial(
        lax.all_to_all, axis_name="tok", split_axis=0, concat_axis=0, tiled=True,
        axis_index_groups=peers,
    )
    parts = swap(held.reshape(rows, spatial)).reshape(timesteps, rows // timesteps, spatial)
    sums = pl.pallas_call(
        earlier_kernel,
        out_shape=jax.ShapeDtypeStruct(parts.shape, BF16),
        in_specs=vmem(1),
        out_specs=vmem(1)[0],
        name="earlier",
    )(parts)
    return swap(sums.reshape(rows, spatial)).reshape(held.shape).astype(F32)


def body(
    initial_guess,
    noise_draws,
    drift_state,
    drift_denoise,
    noise_scale,
    modulation,
    embed_weight,
    space_input,
    space_output,
    time_input,
    time_output,
    final_weight,
):
    timesteps = modulation.shape[0]
    devices = lax.axis_size("tok")
    groups = devices // timesteps
    timestep = lax.axis_index("tok") // groups
    leading = timestep == 0
    own = timestep.astype(jnp.int32).reshape(1)
    if groups == 1:
        step = step_fused
    else:
        peers = [[row * groups + block for block in range(groups)] for row in range(timesteps)]
        step = functools.partial(step_split, peers=peers)
    rates = (drift_state, drift_denoise, noise_scale)
    weights = (
        embed_weight, space_input.T, space_output, time_input.T, time_output, final_weight.T
    )

    def iterate(_, held):
        latent = held[0]
        increment, rounded = step(own, rates, latent, noise_draws, modulation, weights)
        before = sum_before(rounded, timesteps, groups)
        return jnp.where(leading, latent, before), before + increment

    return lax.fori_loop(0, ITERS, iterate, (initial_guess, initial_guess))[1]


def solution(mesh):
    rows = P(("group", "tok"), None, None)
    placed = (rows, rows) + (P(),) * 10
    return jax.shard_map(
        body, mesh=mesh, in_specs=placed, out_specs=rows, check_vma=False
    )
```
